128 devices in a mesh: dp: 64 (over y, x_hi, z, core), mp: 2 (over x_lo).
Axes of the slice: x: 4 (x_hi: 2, x_lo: 2; x = x_hi * 2 + x_lo), y: 4, z: 4, core: 2. Of those that a mesh axis runs over, the one named last changes fastest.
Arguments:
- tokens: bfloat16 [16384, 2048], P('dp'), may hold values from -6 to 6
- cotangent: bfloat16 [16384, 2048], P('dp'), may hold values from -6 to 6
- lengths: int32 [64, 4], P('dp'), may hold values from 0 to 256, as said below
- qkv_weight: float32 [3, 2048, 2048], P(None, 'dp', 'mp'), may hold values from -0.125 to 0.125
- qkv_first: float32 [3, 2048, 2048], P(None, 'dp', 'mp'), may hold values from -112 to 112
- qkv_second: float32 [3, 2048, 2048], P(None, 'dp', 'mp'), may hold values from 638.976 to 10321.92
- dense_weight: float32 [2048, 2048], P(('mp', 'dp')), may hold values from -0.5 to 0.5
- dense_first: float32 [2048, 2048], P(('mp', 'dp')), may hold values from -16 to 16
- dense_second: float32 [2048, 2048], P(('mp', 'dp')), may hold values from 17.2032 to 275.2512
- up_weight: float32 [2048, 8192], P('dp', 'mp'), may hold values from -0.125 to 0.125
- up_first: float32 [2048, 8192], P('dp', 'mp'), may hold values from -24 to 24
- up_second: float32 [2048, 8192], P('dp', 'mp'), may hold values from 39.3216 to 622.592
- down_weight: float32 [8192, 2048], P(('mp', 'dp')), may hold values from -0.0625 to 0.0625
- down_first: float32 [8192, 2048], P(('mp', 'dp')), may hold values from -48 to 48
- down_second: float32 [8192, 2048], P(('mp', 'dp')), may hold values from 121.2416 to 1933.312
- qkv_bias: float32 [3, 2048], P(None, ('mp', 'dp')), may hold values from -3 to 3
- qkv_bias_first: float32 [3, 2048], P(None, ('mp', 'dp')), may hold values from -112 to 112
- qkv_bias_second: float32 [3, 2048], P(None, ('mp', 'dp')), may hold values from 638.976 to 10321.92
- up_bias: float32 [8192], P(('mp', 'dp')), may hold values from -3 to 3
- up_bias_first: float32 [8192], P(('mp', 'dp')), may hold values from -24 to 24
- up_bias_second: float32 [8192], P(('mp', 'dp')), may hold values from 39.3216 to 622.592
- vectors: float32 [4, 2048], P(None, 'dp')
- vector_first: float32 [4, 2048], P(None, 'dp')
- vector_second: float32 [4, 2048], P(None, 'dp')
Outputs:
- output: bfloat16 [16384, 2048], P('dp')
- input_grad: float32 [16384, 2048], P('dp')
- new_qkv_weight: float32 [3, 2048, 2048], P(None, 'dp', 'mp')
- new_qkv_first: float32 [3, 2048, 2048], P(None, 'dp', 'mp')
- new_qkv_second: float32 [3, 2048, 2048], P(None, 'dp', 'mp')
- new_dense_weight: float32 [2048, 2048], P(('mp', 'dp'))
- new_dense_first: float32 [2048, 2048], P(('mp', 'dp'))
- new_dense_second: float32 [2048, 2048], P(('mp', 'dp'))
- new_up_weight: float32 [2048, 8192], P('dp', 'mp')
- new_up_first: float32 [2048, 8192], P('dp', 'mp')
- new_up_second: float32 [2048, 8192], P('dp', 'mp')
- new_down_weight: float32 [8192, 2048], P(('mp', 'dp'))
- new_down_first: float32 [8192, 2048], P(('mp', 'dp'))
- new_down_second: float32 [8192, 2048], P(('mp', 'dp'))
- new_qkv_bias: float32 [3, 2048], P(None, ('mp', 'dp'))
- new_qkv_bias_first: float32 [3, 2048], P(None, ('mp', 'dp'))
- new_qkv_bias_second: float32 [3, 2048], P(None, ('mp', 'dp'))
- new_up_bias: float32 [8192], P(('mp', 'dp'))
- new_up_bias_first: float32 [8192], P(('mp', 'dp'))
- new_up_bias_second: float32 [8192], P(('mp', 'dp'))
- new_vectors: float32 [4, 2048], P(None, 'dp')
- new_vector_first: float32 [4, 2048], P(None, 'dp')
- new_vector_second: float32 [4, 2048], P(None, 'dp')
The draws below stay inside these ranges and needn't reach their ends.
Inputs may be any that keep to these rules, and one draw needn't show every extreme that they name: Each row lists the lengths of up to 4 documents, zeros for absent ones; a row sums to at most 256; the last row is one document of 256 tokens.
All inputs are finite; a program needn't handle non-finite values.
Results may differ from the reference program's by a relative error of at most 0.012.
Values may be sent and summed in bfloat16 or wider, within the bound.
No kernel may reach another device: no remote copies, remote signals or barrier semaphores. Data moves between devices by JAX's collectives and lax.ppermute only.
A program may use at most 512 MiB of HBM per device.

```python
import functools
import math
import jax
import jax.numpy as jnp
from jax import lax

D = 2048
HEADS = 32
HEAD_DIM = 64
ROT_DIMS = 32
FF = 8192
TOK_DEV = 256
DOCS = 4
STEP = 10
SHARDS = 64
TOKENS = 16384


def draw_lengths(key, part):
    key = jax.random.fold_in(key, 1)
    rows = jnp.arange(SHARDS, dtype=jnp.int32)
    least = TOK_DEV // 3
    base = least + (TOK_DEV - least) * rows // max(SHARDS - 1, 1)
    jitter = jax.random.randint(jax.random.fold_in(key, 2), (SHARDS,), 0, TOK_DEV // 8 + 1)
    counts = jnp.maximum(base - jitter, 1)
    counts = jnp.where(rows == SHARDS - 1, TOK_DEV, counts).astype(jnp.int32)
    cuts = jax.random.randint(jax.random.fold_in(key, 3), (SHARDS, DOCS - 1), 0, TOK_DEV + 1)
    cuts = jnp.sort(jnp.minimum(cuts, counts[:, None]), axis=1)
    bounds = jnp.concatenate([jnp.zeros((SHARDS, 1), jnp.int32), cuts.astype(jnp.int32), counts[:, None]], axis=1)
    pieces = bounds[:, 1:] - bounds[:, :-1]
    single = jnp.concatenate([jnp.full((1,), TOK_DEV, jnp.int32), jnp.zeros((DOCS - 1,), jnp.int32)])
    return jnp.where((rows == SHARDS - 1)[:, None], single[None, :], pieces).astype(jnp.int32)


def draw_vectors(key, part):
    key = jax.random.fold_in(key, 11)
    spread = jax.random.uniform(key, (4, D), jnp.float32, -1.0, 1.0)
    gain_row = 1.0 + 0.2 * spread[0:1]
    return jnp.concatenate([gain_row, 0.5 * spread[1:]], axis=0)


def row_factor():
    return jnp.array([5.0, 5.0, 0.67, 0.67], jnp.float32)[:, None]


def draw_vector_first(key, part):
    key = jax.random.fold_in(key, 12)
    sample = jnp.clip(jax.random.normal(key, (4, D), jnp.float32), -6.0, 6.0)
    return 0.111 * jnp.sqrt(row_factor() * TOKENS) * sample


def draw_vector_second(key, part):
    key = jax.random.fold_in(key, 13)
    spread = jnp.exp(jax.random.uniform(key, (4, D), jnp.float32, math.log(0.5), math.log(8.0)))
    return 0.0526 * TOKENS * row_factor() * spread


def levels(own_key, dims, split, low, top_value):
    loudness, own = 1.0, jax.random.fold_in(own_key, 6)
    for dim, blocks in split:
        steps = jnp.exp(jax.random.uniform(jax.random.fold_in(own, dim), (blocks,), jnp.float32, low / len(split), top_value / len(split)))
        loudness = loudness * jnp.repeat(steps, dims[dim] // blocks).reshape([-1 if axis == dim else 1 for axis in range(len(dims))])
    return loudness


def bell_draw(key, extent, scale, limit, shards=(), kind=jnp.bfloat16):
    loudness = levels(key, extent, shards, -0.22, 0.18) if shards else 1.0
    entries = jax.random.normal(key, extent, jnp.float32) * scale * loudness
    return jnp.minimum(jnp.maximum(entries, -limit), limit).astype(kind)


def setup_inputs(seed: int = 0) -> dict:
    splits = jax.random.split(jax.random.key(seed), 25)
    return {
        "tokens": bell_draw(splits[0], (TOKENS, D), 1.0, 6.0, ((0, 64),)),
        "cotangent": bell_draw(splits[1], (TOKENS, D), 1.0, 6.0, ((0, 64),)),
        "lengths": draw_lengths(jax.random.fold_in(splits[24], 71), 0),
        "qkv_weight": bell_draw(splits[3], (3, D, D), D ** -0.5, 0.125, ((1, 64), (2, 2)), jnp.float32),
        "qkv_first": bell_draw(splits[4], (3, D, D), (0.136 * TOKENS ** 0.5), 112.0, ((1, 64), (2, 2)), jnp.float32),
        "qkv_second": jnp.clip(jnp.exp(math.log(10321.92) - 2.7821581 * jax.random.uniform(splits[5], (3, D, D), jnp.float32) ** levels(splits[5], (3, D, D), ((1, 64), (2, 2)), -0.2, 0.2)), 638.976, 10321.92),
        "dense_weight": bell_draw(splits[6], (D, D), (D // 16) ** -0.5, 0.5, ((0, 128),), jnp.float32),
        "dense_first": bell_draw(splits[7], (D, D), (0.022 * TOKENS ** 0.5), 16.0, ((0, 128),), jnp.float32),
        "dense_second": jnp.clip(jnp.exp(math.log(275.2512) - 2.7725887 * jax.random.uniform(splits[8], (D, D), jnp.float32) ** levels(splits[8], (D, D), ((0, 128),), -0.2, 0.2)), 17.2032, 275.2512),
        "up_weight": bell_draw(splits[9], (D, FF), D ** -0.5, 0.125, ((0, 64), (1, 2)), jnp.float32),
        "up_first": bell_draw(splits[10], (D, FF), (0.033 * TOKENS ** 0.5), 24.0, ((0, 64), (1, 2)), jnp.float32),
        "up_second": jnp.clip(jnp.exp(math.log(622.592) - 2.7621173 * jax.random.uniform(splits[11], (D, FF), jnp.float32) ** levels(splits[11], (D, FF), ((0, 64), (1, 2)), -0.2, 0.2)), 39.3216, 622.592),
        "down_weight": bell_draw(splits[12], (FF, D), FF ** -0.5, 0.0625, ((0, 128),), jnp.float32),
        "down_first": bell_draw(splits[13], (FF, D), (0.059 * TOKENS ** 0.5), 48.0, ((0, 128),), jnp.float32),
        "down_second": jnp.clip(jnp.exp(math.log(1933.312) - 2.7692046 * jax.random.uniform(splits[14], (FF, D), jnp.float32) ** levels(splits[14], (FF, D), ((0, 128),), -0.2, 0.2)), 121.2416, 1933.312),
        "qkv_bias": bell_draw(splits[15], (3, D), 0.5, 3.0, ((1, 128),), jnp.float32),
        "qkv_bias_first": bell_draw(splits[16], (3, D), (0.136 * TOKENS ** 0.5), 112.0, ((1, 128),), jnp.float32),
        "qkv_bias_second": jnp.clip(jnp.exp(math.log(10321.92) - 2.7821581 * jax.random.uniform(splits[17], (3, D), jnp.float32) ** levels(splits[17], (3, D), ((1, 128),), -0.2, 0.2)), 638.976, 10321.92),
        "up_bias": bell_draw(splits[18], (FF,), 0.5, 3.0, ((0, 128),), jnp.float32),
        "up_bias_first": bell_draw(splits[19], (FF,), (0.033 * TOKENS ** 0.5), 24.0, ((0, 128),), jnp.float32),
        "up_bias_second": jnp.clip(jnp.exp(math.log(622.592) - 2.7621173 * jax.random.uniform(splits[20], (FF,), jnp.float32) ** levels(splits[20], (FF,), ((0, 128),), -0.2, 0.2)), 39.3216, 622.592),
        "vectors": draw_vectors(jax.random.fold_in(splits[24], 71), 0),
        "vector_first": draw_vector_first(jax.random.fold_in(splits[24], 71), 0),
        "vector_second": draw_vector_second(jax.random.fold_in(splits[24], 71), 0),
    }


@jax.custom_vjp
def low(v):
    return lax.optimization_barrier(v.astype(jnp.bfloat16)).astype(jnp.float32)

@jax.custom_vjp
def low_back(v):
    return v

def low_keep(v):
    return (low(v), None)

def low_pass(kept, grad):
    return (grad,)

def back_keep(v):
    return (v, None)

def back_low(kept, grad):
    return (low(grad),)
low.defvjp(low_keep, low_pass)
low_back.defvjp(back_keep, back_low)
BETA_ONE = 0.9
BETA_TWO = 0.95
ADAM_EPS = 1e-08
WEIGHT_DECAY = 0.1
NORM_EPS = 1e-05
MASKED = -1e+30
GELU_COEF = 0.7978845608028654
HIGHEST = lax.Precision.HIGHEST

def layout(lengths_row, count):
    finish = jnp.cumsum(lengths_row).astype(jnp.int32)
    place = jnp.arange(count, dtype=jnp.int32)
    passed = place[:, None] >= finish[None, :]
    segment = lax.optimization_barrier(jnp.sum(passed.astype(jnp.int32), axis=1)).astype(jnp.int32)
    start = lax.optimization_barrier(jnp.max(jnp.where(passed, finish[None, :], 0), axis=1)).astype(jnp.int32)
    return (segment, place - start, place < finish[-1])

def turning(position, half):
    freq = 10000.0 ** (-2.0 * jnp.arange(half, dtype=jnp.float32) / (2 * half))
    angle = position.astype(jnp.float32)[:, None] * freq[None, :]
    return (jnp.cos(angle)[:, None, :], jnp.sin(angle)[:, None, :])

def rotate(field, cosine, sine, half):
    first = field[..., :half]
    second = field[..., half:2 * half]
    return jnp.concatenate([first * cosine - second * sine, second * cosine + first * sine, field[..., 2 * half:]], axis=-1)

def gelu(value):
    return 0.5 * value * (1.0 + jnp.tanh(GELU_COEF * (value + 0.044715 * value * value * value)))

def attend_row(pieces):
    query, keys, values, segment = pieces
    count = query.shape[0]
    place = jnp.arange(count, dtype=jnp.int32)
    allowed = (segment[:, None] == segment[None, :]) & (place[:, None] >= place[None, :])
    scores = jnp.einsum('qhd,khd->hqk', query, keys, precision=HIGHEST) * HEAD_DIM ** (-0.5)
    scores = low_back(scores)
    scores = jnp.where(allowed[None], scores, MASKED)
    top = lax.optimization_barrier(jnp.max(scores, axis=-1, keepdims=True))
    expo = jnp.exp(scores - top)
    weights = low(expo / lax.optimization_barrier(jnp.sum(expo, axis=-1, keepdims=True)))
    return jnp.einsum('hqk,khd->qhd', weights, values, precision=HIGHEST)

def layer(tokens, params, segment, position):
    qkv_weight, dense_weight, up_weight, down_weight, qkv_bias, up_bias, vectors = [low(item) for item in params]
    rows = tokens.shape[0]
    half = ROT_DIMS // 2
    centered = tokens - lax.optimization_barrier(jnp.mean(tokens, axis=-1, keepdims=True))
    scaled = centered * lax.rsqrt(lax.optimization_barrier(jnp.mean(centered * centered, axis=-1, keepdims=True)) + NORM_EPS)
    normed = low(scaled * vectors[0] + vectors[1])
    joined = jnp.einsum('td,cde->cte', normed, qkv_weight, precision=HIGHEST) + qkv_bias[:, None, :]
    joined = low_back(joined)
    cosine, sine = turning(position, half)
    shaped = joined.reshape(3, rows, HEADS, HEAD_DIM)
    query = low(rotate(shaped[0], cosine, sine, half))
    keys = low(rotate(shaped[1], cosine, sine, half))
    values = low(shaped[2])
    blocks = rows // TOK_DEV
    attended = lax.map(jax.checkpoint(attend_row), (query.reshape(blocks, TOK_DEV, HEADS, HEAD_DIM), keys.reshape(blocks, TOK_DEV, HEADS, HEAD_DIM), values.reshape(blocks, TOK_DEV, HEADS, HEAD_DIM), segment.reshape(blocks, TOK_DEV)))
    mixed = low_back(low(attended.reshape(rows, D)))
    hidden = low_back(jnp.dot(normed, up_weight, precision=HIGHEST) + up_bias)
    active = low(gelu(hidden))
    branch = jnp.dot(mixed, dense_weight, precision=HIGHEST) + jnp.dot(active, down_weight, precision=HIGHEST)
    branch = low_back(branch)
    return tokens + branch + vectors[2] + vectors[3]

def adamw(weight, first, second, grad, rate, decay):
    first = BETA_ONE * first + (1.0 - BETA_ONE) * grad
    second = BETA_TWO * second + (1.0 - BETA_TWO) * grad * grad
    update = first / (1.0 - BETA_ONE ** STEP) / (jnp.sqrt(second / (1.0 - BETA_TWO ** STEP)) + ADAM_EPS)
    return (weight - rate * (update + decay * weight), first, second)

def reference(tokens, cotangent, lengths, qkv_weight, qkv_first, qkv_second, dense_weight, dense_first, dense_second, up_weight, up_first, up_second, down_weight, down_first, down_second, qkv_bias, qkv_bias_first, qkv_bias_second, up_bias, up_bias_first, up_bias_second, vectors, vector_first, vector_second):
    segment, position, valid = jax.vmap(functools.partial(layout, count=TOK_DEV))(lengths)
    per_group = math.gcd(SHARDS, max(1, 4096 // TOK_DEV))
    groups = SHARDS // per_group
    rows = per_group * TOK_DEV

    def whole(source, *params):

        def one_group(pieces):
            return layer(pieces[0], params, pieces[1], pieces[2])
        result = lax.map(jax.checkpoint(one_group), (source.reshape(groups, rows, D), segment.reshape(groups, rows), position.reshape(groups, rows)))
        return result.reshape(TOKENS, D)
    params = (qkv_weight, dense_weight, up_weight, down_weight, qkv_bias, up_bias, vectors)
    output, pullback = jax.vjp(whole, tokens.astype(jnp.float32), *params)
    upstream = cotangent.astype(jnp.float32) * valid.reshape(TOKENS, 1).astype(jnp.float32)
    grads = pullback(upstream)
    new_qkv = adamw(qkv_weight, qkv_first, qkv_second, grads[1], 0.05, WEIGHT_DECAY)
    new_dense = adamw(dense_weight, dense_first, dense_second, grads[2], 0.2, WEIGHT_DECAY)
    new_up = adamw(up_weight, up_first, up_second, grads[3], 0.05, WEIGHT_DECAY)
    new_down = adamw(down_weight, down_first, down_second, grads[4], 0.03, WEIGHT_DECAY)
    new_qkv_bias = adamw(qkv_bias, qkv_bias_first, qkv_bias_second, grads[5], 0.5, 0.0)
    new_up_bias = adamw(up_bias, up_bias_first, up_bias_second, grads[6], 0.5, 0.0)
    new_vectors = adamw(vectors, vector_first, vector_second, grads[7], 0.5, 0.0)
    return (output.astype(jnp.bfloat16), grads[0], new_qkv[0], new_qkv[1], new_qkv[2], new_dense[0], new_dense[1], new_dense[2], new_up[0], new_up[1], new_up[2], new_down[0], new_down[1], new_down[2], new_qkv_bias[0], new_qkv_bias[1], new_qkv_bias[2], new_up_bias[0], new_up_bias[1], new_up_bias[2], new_vectors[0], new_vectors[1], new_vectors[2])
```

```python
import functools
import math

import jax
import jax.numpy as jnp
from jax import lax
from jax.experimental import pallas as pl
from jax.experimental.pallas import tpu as pltpu
from jax.sharding import Mesh, PartitionSpec as P

HEAD_DIM = 64
ROT_DIMS = 32
STEP = 10


BETA_ONE = 0.9
BETA_TWO = 0.95
ADAM_EPS = 1e-08
WEIGHT_DECAY = 0.1
NORM_EPS = 1e-05
MASKED = -1e30
GELU_COEF = 0.7978845608028654

LOW = jnp.bfloat16
WIDE = jnp.float32
RING = 4


def shift(x, axis, step):
    size = lax.axis_size(axis)
    return lax.ppermute(x, axis, [(i, (i + step) % size) for i in range(size)])


def swap(x, axis):
    return shift(x, axis, 1)


def across(x):
    return lax.ppermute(x, ("xh", "mp"), [(0, 3), (3, 0), (1, 2), (2, 1)])


def by_source(index, own, other, dim=0):
    low = jnp.where(index == 0, own, other)
    high = jnp.where(index == 0, other, own)
    return jnp.stack([low, high], axis=dim)


def pick(x, index, dim=0):
    return lax.dynamic_index_in_dim(x, index, dim, keepdims=False)


def put_blocks(blocks, axis):
    me = lax.axis_index(axis)
    out = jnp.zeros((RING,) + blocks[0].shape, blocks[0].dtype)
    for k, block in enumerate(blocks):
        at = (lax.rem(me + k, RING),) + (0,) * block.ndim
        out = lax.dynamic_update_slice(out, block[None], at)
    return out


def gather_direct(x, axis):
    left = shift(x, axis, 1)
    right = shift(x, axis, -1)
    far = shift(x, axis, 2)
    return put_blocks([x, right, far, left], axis)


def gather_ring(x, axis):
    half = x.shape[0] // 2
    left = shift(x, axis, 1)
    right = shift(x, axis, -1)
    far = jnp.concatenate([shift(left[:half], axis, 1), shift(right[half:], axis, -1)])
    return put_blocks([x, right, far, left], axis)


def gather_grid(first, second):
    a = gather_direct(first, "z")
    b = gather_direct(second, "y")
    a = gather_ring(a, "y")
    b = gather_ring(b, "z")
    return a, jnp.swapaxes(b, 0, 1)


def scatter_direct(x, axis):
    me = lax.axis_index(axis)
    own, right, far, left = [pick(x, lax.rem(me + k, RING)) for k in range(RING)]
    from_left = shift(right, axis, 1)
    from_right = shift(left, axis, -1)
    from_far = shift(far, axis, 2)
    return (own.astype(WIDE) + from_left.astype(WIDE)) + (from_right.astype(WIDE) + from_far.astype(WIDE))


def scatter_ring(x, axis):
    me = lax.axis_index(axis)
    own, right, far, left = [pick(x, lax.rem(me + k, RING)) for k in range(RING)]
    half = own.shape[0] // 2
    from_left = shift(jnp.concatenate([far[half:], right[:half]]), axis, 1)
    from_right = shift(jnp.concatenate([far[:half], left[half:]]), axis, -1)
    cut = far.shape[0] - half
    on_right = (right[half:].astype(WIDE) + from_left[:cut].astype(WIDE)).astype(x.dtype)
    on_left = (left[:half].astype(WIDE) + from_right[:half].astype(WIDE)).astype(x.dtype)
    last_left = shift(on_right, axis, 1)
    last_right = shift(on_left, axis, -1)
    top = own[:half].astype(WIDE) + from_left[cut:].astype(WIDE) + last_right.astype(WIDE)
    bottom = own[half:].astype(WIDE) + from_right[half:].astype(WIDE) + last_left.astype(WIDE)
    return jnp.concatenate([top, bottom])


def scatter_grid(first, second):
    a = scatter_ring(first, "y").astype(LOW)
    b = scatter_ring(jnp.swapaxes(second, 0, 1), "z").astype(LOW)
    return scatter_direct(a, "z"), scatter_direct(b, "y")


def attend(joined_ref, bias_ref, d_mixed_ref, start_ref, cos_ref, sin_ref, mixed_ref, d_joined_ref):
    count, width = d_mixed_ref.shape
    heads = width // HEAD_DIM
    lanes = 128
    lane = lax.broadcasted_iota(jnp.int32, (count, lanes), 1) % HEAD_DIM
    cosine = cos_ref[...]
    sine = sin_ref[...]
    half = ROT_DIMS // 2
    low_sine = jnp.where(lane < half, sine, 0.0)
    high_sine = jnp.where((lane >= half) & (lane < ROT_DIMS), sine, 0.0)

    def turn(x, sign):
        up = pltpu.roll(x, half, 1) * high_sine
        down = pltpu.roll(x, lanes - half, 1) * low_sine
        return x * cosine + sign * (up - down)

    place = lax.broadcasted_iota(jnp.int32, (count, count), 0)
    other = lax.broadcasted_iota(jnp.int32, (count, count), 1)
    allowed = (other >= start_ref[...]) & (other <= place)
    scale = HEAD_DIM ** (-0.5)

    def dot(a, b, da, db):
        return lax.dot_general(a, b, (((da,), (db,)), ((), ())), preferred_element_type=WIDE)

    for pair in range(width // lanes):
        at = pair * lanes
        query2 = turn(joined_ref[:, at : at + lanes] + bias_ref[:, at : at + lanes], 1.0).astype(LOW)
        k_at = width + at
        keys2 = turn(joined_ref[:, k_at : k_at + lanes] + bias_ref[:, k_at : k_at + lanes], 1.0).astype(LOW)
        v_at = 2 * width + at
        values2 = (joined_ref[:, v_at : v_at + lanes] + bias_ref[:, v_at : v_at + lanes]).astype(LOW)
        d_out2 = d_mixed_ref[:, at : at + lanes]
        mixed, d_query, d_keys, d_values = [], [], [], []
        for h in range(lanes // HEAD_DIM):
            cut = slice(h * HEAD_DIM, (h + 1) * HEAD_DIM)
            query, keys, values, d_out = query2[:, cut], keys2[:, cut], values2[:, cut], d_out2[:, cut]
            scores = jnp.where(allowed, dot(query, keys, 1, 1) * scale, MASKED)
            expo = jnp.exp(scores - jnp.max(scores, axis=1, keepdims=True))
            weights = expo / jnp.sum(expo, axis=1, keepdims=True)
            weights_low = weights.astype(LOW)
            mixed.append(dot(weights_low, values, 1, 0))
            d_weights = dot(d_out, values, 1, 1)
            d_values.append(dot(weights_low, d_out, 0, 0))
            delta = jnp.sum(weights * d_weights, axis=1, keepdims=True)
            d_scores = (weights * (d_weights - delta)).astype(LOW)
            d_query.append(dot(d_scores, keys, 1, 0) * scale)
            d_keys.append(dot(d_scores, query, 0, 0) * scale)
        mixed_ref[:, at : at + lanes] = jnp.concatenate(mixed, axis=1).astype(LOW)
        d_joined_ref[:, at : at + lanes] = turn(jnp.concatenate(d_query, axis=1), -1.0).astype(LOW)
        d_joined_ref[:, k_at : k_at + lanes] = turn(jnp.concatenate(d_keys, axis=1), -1.0).astype(LOW)
        d_joined_ref[:, v_at : v_at + lanes] = jnp.concatenate(d_values, axis=1).astype(LOW)


def attention(joined, bias, d_mixed, start, cosine, sine, count):
    rows, width = d_mixed.shape

    def block(columns):
        return pl.BlockSpec((count, columns), lambda r: (r, 0))

    return pl.pallas_call(
        attend,
        grid=(rows // count,),
        in_specs=[
            block(3 * width),
            pl.BlockSpec((1, 3 * width), lambda r: (0, 0)),
            block(width),
            block(1),
            block(128),
            block(128),
        ],
        out_specs=[block(width), block(3 * width)],
        out_shape=[
            jax.ShapeDtypeStruct((rows, width), LOW),
            jax.ShapeDtypeStruct((rows, 3 * width), LOW),
        ],
        compiler_params=pltpu.CompilerParams(vmem_limit_bytes=32 * 1024 * 1024),
        cost_estimate=pl.CostEstimate(flops=2 * 7 * rows * count * width, bytes_accessed=rows * width * 16, transcendentals=0),
    )(joined, bias, d_mixed, start, cosine, sine)


def starts(lengths_row, count):
    finish = jnp.cumsum(lengths_row)
    place = jnp.arange(count, dtype=jnp.int32)
    passed = place[:, None] >= finish[None, :]
    start = jnp.max(jnp.where(passed, finish[None, :], 0), axis=1)
    return start, place < finish[-1]


def gelu(value):
    return 0.5 * value * (1.0 + jnp.tanh(GELU_COEF * (value + 0.044715 * value * value * value)))


def gelu_slope(value):
    inner = jnp.tanh(GELU_COEF * (value + 0.044715 * value * value * value))
    return 0.5 * (1.0 + inner) + 0.5 * value * (1.0 - inner * inner) * GELU_COEF * (
        1.0 + 3.0 * 0.044715 * value * value
    )


def adamw(weight, first, second, grad, rate, decay):
    first = BETA_ONE * first + (1.0 - BETA_ONE) * grad
    second = BETA_TWO * second + (1.0 - BETA_TWO) * grad * grad
    update = first / (1.0 - BETA_ONE**STEP) / (jnp.sqrt(second / (1.0 - BETA_TWO**STEP)) + ADAM_EPS)
    return (weight - rate * (update + decay * weight), first, second)


def rows_of_group(x):
    xh, c = lax.axis_index("xh"), lax.axis_index("c")
    both = by_source(xh, x, across(x))
    return by_source(c, both, swap(both, "c"), 1)


def sum_to_owner(partial):
    xh, c = lax.axis_index("xh"), lax.axis_index("c")
    mine = pick(partial, c, 1).astype(WIDE) + swap(pick(partial, 1 - c, 1), "c").astype(WIDE)
    mine = mine.astype(LOW)
    own = pick(mine, xh).astype(WIDE) + across(pick(mine, 1 - xh)).astype(WIDE)
    own = own.astype(LOW)
    return own.astype(WIDE) + swap(own, "mp").astype(WIDE)


def local(
    tokens,
    cotangent,
    lengths,
    qkv_weight,
    qkv_first,
    qkv_second,
    dense_weight,
    dense_first,
    dense_second,
    up_weight,
    up_first,
    up_second,
    down_weight,
    down_first,
    down_second,
    qkv_bias,
    qkv_bias_first,
    qkv_bias_second,
    up_bias,
    up_bias_first,
    up_bias_second,
    vectors,
    vector_first,
    vector_second,
):
    xh, c = lax.axis_index("xh"), lax.axis_index("c")
    count, model = tokens.shape
    part = qkv_weight.shape[1]
    own_units = down_weight.shape[0]
    own_rows = dense_weight.shape[0]
    heads_width = 2 * 128
    units = 16 * own_units

    own_start, own_valid = starts(lengths[0], count)
    upstream = cotangent.astype(WIDE) * own_valid[:, None].astype(WIDE)
    all_tokens = rows_of_group(tokens).reshape(4 * count, model)
    all_back = rows_of_group(upstream.astype(LOW)).reshape(4 * count, model)
    all_lengths = rows_of_group(lengths[0]).reshape(4, -1)

    q = qkv_weight.astype(LOW).reshape(3, part, 2, 2, 2, 128)
    q = q.transpose(4, 2, 1, 0, 3, 5).reshape(2, 2, part, 3 * heads_width)
    u = up_weight.astype(LOW).reshape(part, 4, 2, 4, 2, own_units)
    u = u.transpose(2, 4, 0, 1, 3, 5).reshape(2, 2, part, units)
    cut = jnp.concatenate([q, u], axis=-1)
    cut = by_source(xh, pick(cut, xh), swap(pick(cut, 1 - xh), "xh"))
    cut = by_source(c, pick(cut, c, 1), swap(pick(cut, 1 - c, 1), "c"), 1)
    cut = cut.reshape(4 * part, 3 * heads_width + units)

    small = vectors.astype(LOW).reshape(-1)
    small = by_source(xh, small, swap(small, "xh")).reshape(-1)
    small = jnp.concatenate([small, qkv_bias.astype(LOW).reshape(-1)])
    small = by_source(c, small, swap(small, "c")).reshape(-1)
    small = jnp.concatenate([small, up_bias.astype(LOW)])
    n_small = small.shape[0]
    lines = 2 * own_rows
    small = jnp.pad(small, (0, lines * 256 - n_small)).reshape(lines, 256)
    dense_lines = dense_weight.astype(LOW).reshape(own_rows, 8, 256).transpose(1, 0, 2).reshape(8 * own_rows, 256)

    first = cut[:, : 2 * heads_width]
    second = jnp.concatenate([cut[:, 2 * heads_width : 3 * heads_width], dense_lines, small])
    first, second = gather_grid(first, second)
    up_all, down_all = gather_grid(cut[:, 3 * heads_width :], down_weight.astype(LOW))

    def natural(x):
        return x.reshape(4, 4, 2, 2 * part, -1).transpose(0, 2, 1, 3, 4).reshape(model, -1)

    w_qkv = jnp.concatenate([natural(first), natural(second[:, :, : 4 * part])], axis=1)
    w_up = natural(up_all)
    w_down = down_all.reshape(units, model)
    dense_all = second[:, :, 4 * part : 4 * part + 8 * own_rows].reshape(4, 4, 8, own_rows, 256)
    dense_all = dense_all.transpose(0, 1, 3, 2, 4).reshape(2, 2, 4, own_rows, model)
    w_dense = by_source(c, pick(dense_all, c), swap(pick(dense_all, 1 - c), "c"), 2)
    w_dense = w_dense.reshape(heads_width, model)

    small = second[:, :, 4 * part + 8 * own_rows :].reshape(4, 4, -1)[:, :, :n_small].astype(WIDE)
    n_vec = 4 * vectors.shape[1]
    n_bias = 3 * qkv_bias.shape[1]
    per_core = 2 * n_vec + n_bias
    cores = small[:, :, : 2 * per_core].reshape(4, 4, 2, per_core)
    gains = cores[..., : 2 * n_vec].reshape(4, 4, 2, 2, 4, -1).transpose(4, 0, 3, 1, 2, 5).reshape(4, model)
    b_qkv = cores[..., 2 * n_vec :].reshape(2, 2, 4, 2, 3, -1)
    b_qkv = pick(b_qkv, c).transpose(3, 0, 1, 2, 4).reshape(1, 3 * heads_width)
    b_up = small[:, :, 2 * per_core :].reshape(units)

    def scale_rows(x):
        source = x.astype(WIDE)
        centered = source - jnp.mean(source, axis=-1, keepdims=True)
        inverse = lax.rsqrt(jnp.mean(centered * centered, axis=-1, keepdims=True) + NORM_EPS)
        return centered * inverse, inverse

    scaled, _ = scale_rows(all_tokens)
    normed = (scaled * gains[0] + gains[1]).astype(LOW)

    start, _ = jax.vmap(functools.partial(starts, count=count))(all_lengths)
    position = (jnp.arange(count, dtype=jnp.int32)[None, :] - start).reshape(-1, 1)
    start = start.reshape(-1, 1)
    half = ROT_DIMS // 2
    lane = jnp.arange(128, dtype=jnp.int32) % HEAD_DIM
    freq = 10000.0 ** (-2.0 * (lane % half).astype(WIDE) / (2 * half))
    angle = position.astype(WIDE) * freq[None, :]
    turned = (lane < ROT_DIMS)[None, :]
    cosine = jnp.where(turned, jnp.cos(angle), 1.0)
    sine = jnp.where(turned, jnp.sin(angle), 0.0)

    def dot(a, b, da, db):
        return lax.dot_general(a, b, (((da,), (db,)), ((), ())), preferred_element_type=WIDE)

    d_mixed = dot(all_back, w_dense, 1, 1).astype(LOW)
    joined = dot(normed, w_qkv, 1, 0)
    mixed, d_joined = attention(joined, b_qkv, d_mixed, start, cosine, sine, count)
    grad_qkv = dot(normed, d_joined, 0, 0)
    grad_qkv_bias = jnp.sum(d_joined.astype(WIDE), axis=0)
    grad_dense = dot(mixed, all_back, 0, 0)

    d_active = dot(all_back, w_down, 1, 1)
    hidden = dot(normed, w_up, 1, 0) + b_up
    active = gelu(hidden).astype(LOW)
    d_hidden = (d_active * gelu_slope(hidden)).astype(LOW)
    d_normed_part = dot(d_joined, w_qkv, 1, 1) + dot(d_hidden, w_up, 1, 1)
    d_normed = sum_to_owner(d_normed_part.astype(LOW).reshape(2, 2, count, model))
    branch_part = dot(mixed, w_dense, 1, 0) + dot(active, w_down, 1, 0)
    branch = sum_to_owner(branch_part.astype(LOW).reshape(2, 2, count, model))
    grad_up = dot(normed, d_hidden, 0, 0)
    grad_up_bias = jnp.sum(d_hidden.astype(WIDE), axis=0)
    grad_down = dot(active, all_back, 0, 0)

    def blocks(x):
        return x.reshape(4, 2, 4, 2 * part, -1).transpose(0, 2, 1, 3, 4).reshape(4, 4, 4 * part, -1)

    gq = blocks(grad_qkv.astype(LOW))
    gd = grad_dense.astype(LOW).reshape(2, 4, 2, own_rows, model)
    other = swap(pick(gd, 1 - c, 2), "c")
    gd = by_source(c, pick(gd, c, 2), other).reshape(4, 4, own_rows, 8, 256)
    gd = gd.transpose(0, 1, 3, 2, 4).reshape(4, 4, 8 * own_rows, 256)
    first, second = scatter_grid(
        gq[..., : 2 * heads_width], jnp.concatenate([gq[..., 2 * heads_width :], gd], axis=2)
    )
    own_up, own_down = scatter_grid(
        blocks(grad_up.astype(LOW)), grad_down.astype(LOW).reshape(4, 4, own_units, model)
    )
    owned_dense = second[4 * part :].reshape(8, own_rows, 256).transpose(1, 0, 2).reshape(own_rows, model)
    back_cut = jnp.concatenate([first, second[: 4 * part], own_up], axis=1).astype(LOW)
    back_cut = back_cut.reshape(2, 2, part, 3 * heads_width + units)
    back_cut = by_source(c, pick(back_cut, c, 1), swap(pick(back_cut, 1 - c, 1), "c"), 1)
    back_cut = by_source(xh, pick(back_cut, xh), swap(pick(back_cut, 1 - xh), "xh")).astype(WIDE)
    owned_qkv = back_cut[..., : 3 * heads_width].reshape(2, 2, part, 3, 2, 128)
    owned_qkv = owned_qkv.transpose(3, 2, 1, 4, 0, 5).reshape(qkv_weight.shape)
    owned_up = back_cut[..., 3 * heads_width :].reshape(2, 2, part, 4, 4, own_units)
    owned_up = owned_up.transpose(2, 3, 0, 4, 1, 5).reshape(up_weight.shape)

    column_sum = jnp.sum(upstream, axis=0)
    gv_part = jnp.stack([jnp.sum(d_normed_part * scaled, axis=0), jnp.sum(d_normed_part, axis=0)])
    gv_part = jnp.concatenate([gv_part, 0.5 * column_sum[None]])
    gv = gv_part.reshape(3, 4, 2, 4, 2, part)
    gb = grad_qkv_bias.reshape(3, 2, 4, 2, -1)
    n_gb = gb.size // 2
    sent = jnp.concatenate([pick(gv, 1 - c, 4).reshape(-1), pick(gb, 1 - c, 3).reshape(-1)])
    got = swap(sent, "c")
    n_gv = gv.size // 2
    gv = pick(gv, c, 4) + got[:n_gv].reshape(3, 4, 2, 4, part)
    gb_own = pick(gb, c, 3)
    gb = by_source(c, gb_own, got[n_gv:].reshape(gb_own.shape), 1)
    gv = pick(gv, xh, 2) + swap(pick(gv, 1 - xh, 2), "xh")
    gv = gv + swap(gv, "mp")
    pack = jnp.concatenate(
        [
            gv.transpose(1, 2, 0, 3).reshape(4, 4, -1),
            gb.reshape(3, 4, 4, -1).transpose(1, 2, 0, 3).reshape(4, 4, -1),
            grad_up_bias.reshape(4, 4, -1),
        ],
        axis=2,
    )
    n_pack = pack.shape[2]
    pack = jnp.pad(pack, ((0, 0), (0, 0), (0, 256 - n_pack)))
    pack = scatter_direct(scatter_direct(pack, "y"), "z")
    n_v = 3 * part
    got_vectors = pack[:n_v].reshape(3, part)
    owned_vectors = jnp.concatenate([got_vectors, got_vectors[2:]])
    owned_qkv_bias = pack[n_v : n_v + n_bias].reshape(qkv_bias.shape)
    owned_up_bias = pack[n_v + n_bias : n_pack]

    own_scaled, inverse = scale_rows(tokens)
    output = (tokens.astype(WIDE) + branch + gains[2] + gains[3]).astype(LOW)
    d_scaled = d_normed * gains[0]
    input_grad = upstream + inverse * (
        d_scaled
        - jnp.mean(d_scaled, axis=-1, keepdims=True)
        - own_scaled * jnp.mean(d_scaled * own_scaled, axis=-1, keepdims=True)
    )

    new_qkv = adamw(qkv_weight, qkv_first, qkv_second, owned_qkv, 0.05, WEIGHT_DECAY)
    new_dense = adamw(dense_weight, dense_first, dense_second, owned_dense, 0.2, WEIGHT_DECAY)
    new_up = adamw(up_weight, up_first, up_second, owned_up, 0.05, WEIGHT_DECAY)
    new_down = adamw(down_weight, down_first, down_second, own_down, 0.03, WEIGHT_DECAY)
    new_qkv_bias = adamw(qkv_bias, qkv_bias_first, qkv_bias_second, owned_qkv_bias, 0.5, 0.0)
    new_up_bias = adamw(up_bias, up_bias_first, up_bias_second, owned_up_bias, 0.5, 0.0)
    new_vectors = adamw(vectors, vector_first, vector_second, owned_vectors, 0.5, 0.0)
    return (output, input_grad, *new_qkv, *new_dense, *new_up, *new_down, *new_qkv_bias, *new_up_bias, *new_vectors)


def solution(mesh):
    mesh = Mesh(mesh.devices.reshape(4, 2, 4, 2, 2), ("y", "xh", "z", "c", "mp"))
    dp = ("y", "xh", "z", "c")
    both = ("mp",) + dp
    weights = (P(None, dp, "mp"),) * 3 + (P(both, None),) * 3 + (P(dp, "mp"),) * 3 + (P(both, None),) * 3
    smalls = (P(None, both),) * 3 + (P(both),) * 3 + (P(None, dp),) * 3
    rows = P(dp, None)
    in_specs = (rows, rows, rows) + weights + smalls
    out_specs = (rows, rows) + weights + smalls
    return jax.shard_map(local, mesh=mesh, in_specs=in_specs, out_specs=out_specs, check_vma=False)
```

```python
import functools
import math

import jax
import jax.numpy as jnp
from jax import lax
from jax.experimental import pallas as pl
from jax.experimental.pallas import tpu as pltpu
from jax.sharding import Mesh, PartitionSpec as P

HEAD_DIM = 64
ROT_DIMS = 32
STEP = 10


BETA_ONE = 0.9
BETA_TWO = 0.95
ADAM_EPS = 1e-08
WEIGHT_DECAY = 0.1
NORM_EPS = 1e-05
MASKED = -1e30
GELU_COEF = 0.7978845608028654

LOW = jnp.bfloat16
WIDE = jnp.float32
RING = 4
MICROSECOND = 1100000000


def shift(x, axis, step):
    size = lax.axis_size(axis)
    return lax.ppermute(x, axis, [(i, (i + step) % size) for i in range(size)])


def swap(x, axis):
    return shift(x, axis, 1)


def across(x):
    return lax.ppermute(x, ("xh", "mp"), [(0, 3), (3, 0), (1, 2), (2, 1)])


def by_source(index, own, other, dim=0):
    low = jnp.where(index == 0, own, other)
    high = jnp.where(index == 0, other, own)
    return jnp.stack([low, high], axis=dim)


def pick(x, index, dim=0):
    return lax.dynamic_index_in_dim(x, index, dim, keepdims=False)


def wide_sum(*xs):
    return functools.reduce(lambda a, b: a + b, [x.astype(WIDE) for x in xs])


def scatter_direct(x, axis):
    me = lax.axis_index(axis)
    own, right, far, left = [pick(x, lax.rem(me + k, RING)) for k in range(RING)]
    return wide_sum(own, shift(right, axis, 1), shift(left, axis, -1), shift(far, axis, 2))


def scatter_first(x, axis):
    flat = x.reshape((2 * RING,) + x.shape[2:])
    return shift(flat[3:5], axis, 1), shift(flat[5:7], axis, -1)


def scatter_last(x, got, axis):
    from_left, from_right = got
    on_right = wide_sum(x[1, 0], from_left[1]).astype(LOW)
    on_left = wide_sum(x[3, 1], from_right[0]).astype(LOW)
    return shift(on_right, axis, 1), shift(on_left, axis, -1)


def scatter_join(x, got, last, kind=LOW):
    from_left, from_right = got
    top = wide_sum(x[0, 0], from_right[1], last[0])
    bottom = wide_sum(x[0, 1], from_left[0], last[1])
    return jnp.stack([top, bottom]).astype(kind)


def dot(a, b, da, db):
    return lax.dot_general(a, b, (((da,), (db,)), ((), ())), preferred_element_type=WIDE)


def call(kernel, grid, in_specs, out_specs, out_shape, args, flops=0, limit=48, scratch=()):
    moved = sum(a.size * a.dtype.itemsize for a in args) if flops > 1 else 1
    return pl.pallas_call(
        kernel,
        grid=grid,
        in_specs=in_specs,
        out_specs=out_specs,
        out_shape=out_shape,
        scratch_shapes=scratch,
        compiler_params=pltpu.CompilerParams(vmem_limit_bytes=limit * 1024 * 1024),
        cost_estimate=pl.CostEstimate(flops=flops, bytes_accessed=moved, transcendentals=0),
    )(*args)


def call_at(kernel, place, grid, in_specs, out_specs, out_shape, args, flops=0, limit=56):
    moved = sum(a.size * a.dtype.itemsize for a in args) if flops > 1 else 1
    return pl.pallas_call(
        kernel,
        grid_spec=pltpu.PrefetchScalarGridSpec(num_scalar_prefetch=1, grid=grid, in_specs=in_specs, out_specs=out_specs),
        out_shape=out_shape,
        compiler_params=pltpu.CompilerParams(vmem_limit_bytes=limit * 1024 * 1024),
        cost_estimate=pl.CostEstimate(flops=flops, bytes_accessed=moved, transcendentals=0),
    )(place, *args)


def struct(shape, dtype):
    return jax.ShapeDtypeStruct(shape, dtype)


def full(*shape):
    return pl.BlockSpec(shape, lambda *i: (0,) * len(shape))


PLACES = [((y * 2 + xh) * 4 + z, (y * 4 + z) * 2 + xh) for y in range(4) for xh in range(2) for z in range(4)]
HERE = [here for here, _ in sorted(PLACES, key=lambda p: p[1])]
THERE = [there for _, there in sorted(PLACES)]


def reorder(x, order):
    return jnp.concatenate([x[:, 64 * k : 64 * (k + 1)] for k in order], axis=1)


def cut_columns(qkv_ref, up_ref, out_ref):
    for xh in range(2):
        for c in range(2):
            to = xh * 2 + c
            for w in range(3):
                for low in range(2):
                    at = (2 * c + low) * 256 + xh * 128
                    out_ref[to, :, w * 256 + low * 128 : w * 256 + (low + 1) * 128] = qkv_ref[w, :, at : at + 128].astype(LOW)
            for pair in range(8):
                y, z = pair // 2, 2 * (pair % 2)
                at = y * 1024 + xh * 512 + z * 128 + c * 64
                piece = jnp.concatenate([up_ref[:, at : at + 64], up_ref[:, at + 128 : at + 192]], axis=1)
                out_ref[to, :, 768 + pair * 128 : 768 + (pair + 1) * 128] = piece.astype(LOW)


def normalise(x):
    centered = x - jnp.mean(x, axis=-1, keepdims=True)
    inverse = lax.rsqrt(jnp.mean(centered * centered, axis=-1, keepdims=True) + NORM_EPS)
    return centered * inverse, inverse


def norm_rows(pair_ref, other_ref, gains_ref, normed_ref, scaled_ref, turned_ref):
    def run(ref):
        scaled, _ = normalise(ref[0].astype(WIDE))
        normed = reorder(scaled * gains_ref[0:1] + gains_ref[1:2], HERE)
        normed_ref[...] = normed.astype(LOW)
        scaled_ref[...] = reorder(scaled, HERE).astype(LOW)
        for k in range(8):
            turned_ref[k * 256 : (k + 1) * 256, :] = normed[:, k * 256 : (k + 1) * 256].T.astype(LOW)

    pl.when(pl.program_id(0) < 2)(lambda: run(pair_ref))
    pl.when(pl.program_id(0) >= 2)(lambda: run(other_ref))


def project(normed_ref, back_ref, weight_ref, dense_ref, joined_ref, d_mixed_ref):
    joined_ref[...] = dot(normed_ref[...], weight_ref[...].reshape(normed_ref.shape[1], -1), 1, 0)

    @pl.when(pl.program_id(0) == 0)
    def _():
        dense = jnp.concatenate([dense_ref[k] for k in range(8)], axis=1)
        d_mixed_ref[...] = dot(back_ref[...], dense, 1, 1).astype(LOW)


def attention_grads(place_ref, turned_ref, d_joined_ref, mixed_ref, back_ref, grad_ref, dense_ref, bias_ref):
    step = pl.program_id(0)
    to_y = lax.rem(step // 2 - place_ref[0] + 4, 4)
    grad_ref[to_y, lax.rem(step, 2)] = dot(turned_ref[...], d_joined_ref[...], 1, 0).astype(LOW)
    dense_ref[0] = dot(mixed_ref[...], back_ref[...], 0, 0).astype(LOW)

    @pl.when(step == 0)
    def _():
        bias_ref[...] = jnp.sum(d_joined_ref[...].astype(WIDE), axis=0, keepdims=True)


def feed_forward(
    normed_ref, turned_ref, back_ref, up_ref, down_a_ref, down_b_ref, bias_ref, active_ref, d_hidden_ref, grad_ref, d_bias_ref
):
    step = pl.program_id(0)
    model = normed_ref.shape[1]
    half = model // 2
    width = active_ref.shape[1]
    hidden = dot(normed_ref[...], up_ref[...].reshape(model, width), 1, 0) + bias_ref[...]
    down = jnp.concatenate([down_a_ref[...].reshape(width, half), down_b_ref[...].reshape(width, half)], axis=1)
    d_active = dot(back_ref[...], down, 1, 1)
    square = hidden * hidden
    inner = jnp.tanh(GELU_COEF * (hidden + 0.044715 * square * hidden))
    ends = 0.5 * (1.0 + inner)
    active = (hidden * ends).astype(LOW)
    slope = ends + 0.5 * hidden * (1.0 - inner * inner) * GELU_COEF * (1.0 + 3.0 * 0.044715 * square)
    d_hidden = (d_active * slope).astype(LOW)
    active_ref[...] = active
    d_hidden_ref[...] = d_hidden
    d_bias_ref[...] = jnp.sum(d_hidden.astype(WIDE), axis=0, keepdims=True)
    column = pl.multiple_of(step * width, width)
    up_grad = dot(turned_ref[...], d_hidden, 1, 0).astype(LOW)
    for k in range(16):
        grad_ref[k, :128, pl.ds(column, width)] = up_grad[k * 128 : (k + 1) * 128]
    down_grad = dot(active, back_ref[...], 0, 0).astype(LOW)
    for z in range(4):
        grad_ref[step * 4 + z, 128:192] = down_grad[z * 64 : (z + 1) * 64, :half]
        grad_ref[step * 4 + z, 192:256] = down_grad[z * 64 : (z + 1) * 64, half:]


def branch_parts(mixed_ref, active_ref, dense_ref, down_ref, keep_ref, send_ref):
    branch = dot(mixed_ref[...], dense_ref[0], 1, 0)
    branch += dot(active_ref[...], down_ref[...].reshape(active_ref.shape[1], -1), 1, 0)
    branch = branch.astype(LOW)
    half = branch.shape[0] // 2
    keep_ref[...] = branch[:half]
    send_ref[...] = branch[half:]


def normed_parts(d_joined_ref, d_hidden_ref, scaled_ref, qkv_ref, up_ref, keep_ref, send_ref, sums_ref):
    half, width = keep_ref.shape
    total = dot(d_joined_ref[...], qkv_ref[...].reshape(width, -1)[:, : d_joined_ref.shape[1]], 1, 1)
    total += dot(d_hidden_ref[...], up_ref[...].reshape(width, -1), 1, 1)
    low = total.astype(LOW)
    keep_ref[...] = low[:half]
    send_ref[...] = low[half:]
    sums_ref[0:1] = jnp.sum(total * scaled_ref[...].astype(WIDE), axis=0, keepdims=True)
    sums_ref[1:2] = jnp.sum(total, axis=0, keepdims=True)


def input_rows(tokens_ref, cotangent_ref, valid_ref, d_one_ref, d_two_ref, gains_ref, grad_ref):
    scaled, inverse = normalise(tokens_ref[...].astype(WIDE))
    upstream = cotangent_ref[...].astype(WIDE) * valid_ref[...]
    d_normed = reorder(d_one_ref[...].astype(WIDE) + d_two_ref[...].astype(WIDE), THERE)
    d_scaled = d_normed * gains_ref[0:1]
    grad_ref[...] = upstream + inverse * (
        d_scaled
        - jnp.mean(d_scaled, axis=-1, keepdims=True)
        - scaled * jnp.mean(d_scaled * scaled, axis=-1, keepdims=True)
    )


def update_qkv(grad_ref, weight_ref, first_ref, second_ref, *out_refs):
    for xh in range(2):
        for y in range(4):
            for w in range(3):
                at = slice(y * 256 + xh * 128, y * 256 + (xh + 1) * 128)
                here = w * 256 + (y % 2) * 128
                grad = grad_ref[xh * 2 + y // 2, :, here : here + 128].astype(WIDE)
                new = adamw(weight_ref[w, :, at], first_ref[w, :, at], second_ref[w, :, at], grad, 0.05, WEIGHT_DECAY)
                for ref, value in zip(out_refs, new):
                    ref[w, :, at] = value


def update_up(grad_ref, weight_ref, first_ref, second_ref, *out_refs):
    for xh in range(2):
        for y in range(4):
            for z in range(4):
                base = y * 1024 + xh * 512 + z * 128
                at = slice(base, base + 128)
                here = (y * 4 + z) * 64
                grad = jnp.concatenate(
                    [grad_ref[xh * 2 + c, :, here : here + 64].astype(WIDE) for c in range(2)], axis=1
                )
                new = adamw(weight_ref[:, at], first_ref[:, at], second_ref[:, at], grad, 0.05, WEIGHT_DECAY)
                for ref, value in zip(out_refs, new):
                    ref[:, at] = value


def held(*xs):
    return lax.optimization_barrier(xs)


def attend(joined_ref, bias_ref, d_mixed_ref, start_ref, cos_ref, sin_ref, mixed_ref, d_joined_ref):
    count, width = d_mixed_ref.shape
    heads = width // HEAD_DIM
    lanes = 128
    lane = lax.broadcasted_iota(jnp.int32, (count, lanes), 1) % HEAD_DIM
    cosine = cos_ref[...]
    sine = sin_ref[...]
    half = ROT_DIMS // 2
    low_sine = jnp.where(lane < half, sine, 0.0)
    high_sine = jnp.where((lane >= half) & (lane < ROT_DIMS), sine, 0.0)

    def turn(x, sign):
        up = pltpu.roll(x, half, 1) * high_sine
        down = pltpu.roll(x, lanes - half, 1) * low_sine
        return x * cosine + sign * (up - down)

    place = lax.broadcasted_iota(jnp.int32, (count, count), 0)
    other = lax.broadcasted_iota(jnp.int32, (count, count), 1)
    allowed = (other >= start_ref[...]) & (other <= place)
    scale = HEAD_DIM ** (-0.5)

    def dot(a, b, da, db):
        return lax.dot_general(a, b, (((da,), (db,)), ((), ())), preferred_element_type=WIDE)

    for pair in range(width // lanes):
        at = pair * lanes
        query2 = turn(joined_ref[:, at : at + lanes] + bias_ref[:, at : at + lanes], 1.0).astype(LOW)
        k_at = width + at
        keys2 = turn(joined_ref[:, k_at : k_at + lanes] + bias_ref[:, k_at : k_at + lanes], 1.0).astype(LOW)
        v_at = 2 * width + at
        values2 = (joined_ref[:, v_at : v_at + lanes] + bias_ref[:, v_at : v_at + lanes]).astype(LOW)
        d_out2 = d_mixed_ref[:, at : at + lanes]
        mixed, d_query, d_keys, d_values = [], [], [], []
        for h in range(lanes // HEAD_DIM):
            cut = slice(h * HEAD_DIM, (h + 1) * HEAD_DIM)
            query, keys, values, d_out = query2[:, cut], keys2[:, cut], values2[:, cut], d_out2[:, cut]
            scores = jnp.where(allowed, dot(query, keys, 1, 1) * scale, MASKED)
            expo = jnp.exp(scores - jnp.max(scores, axis=1, keepdims=True))
            weights = expo / jnp.sum(expo, axis=1, keepdims=True)
            weights_low = weights.astype(LOW)
            mixed.append(dot(weights_low, values, 1, 0))
            d_weights = dot(d_out, values, 1, 1)
            d_values.append(dot(weights_low, d_out, 0, 0))
            delta = jnp.sum(weights * d_weights, axis=1, keepdims=True)
            d_scores = (weights * (d_weights - delta)).astype(LOW)
            d_query.append(dot(d_scores, keys, 1, 0) * scale)
            d_keys.append(dot(d_scores, query, 0, 0) * scale)
        mixed_ref[:, at : at + lanes] = jnp.concatenate(mixed, axis=1).astype(LOW)
        d_joined_ref[:, at : at + lanes] = turn(jnp.concatenate(d_query, axis=1), -1.0).astype(LOW)
        d_joined_ref[:, k_at : k_at + lanes] = turn(jnp.concatenate(d_keys, axis=1), -1.0).astype(LOW)
        d_joined_ref[:, v_at : v_at + lanes] = jnp.concatenate(d_values, axis=1).astype(LOW)


def attention(joined, bias, d_mixed, start, cosine, sine, count):
    rows, width = d_mixed.shape

    def block(columns):
        return pl.BlockSpec((count, columns), lambda r: (r, 0))

    return pl.pallas_call(
        attend,
        grid=(rows // count,),
        in_specs=[
            block(3 * width),
            pl.BlockSpec((1, 3 * width), lambda r: (0, 0)),
            block(width),
            block(1),
            block(128),
            block(128),
        ],
        out_specs=[block(width), block(3 * width)],
        out_shape=[
            jax.ShapeDtypeStruct((rows, width), LOW),
            jax.ShapeDtypeStruct((rows, 3 * width), LOW),
        ],
        compiler_params=pltpu.CompilerParams(vmem_limit_bytes=32 * 1024 * 1024),
        cost_estimate=pl.CostEstimate(flops=16 * MICROSECOND, bytes_accessed=rows * width * 16, transcendentals=0),
    )(joined, bias, d_mixed, start, cosine, sine)


def starts(lengths_row, count):
    finish = jnp.cumsum(lengths_row)
    place = jnp.arange(count, dtype=jnp.int32)
    passed = place[:, None] >= finish[None, :]
    start = jnp.max(jnp.where(passed, finish[None, :], 0), axis=1)
    return start, place < finish[-1]


def gelu(value):
    return 0.5 * value * (1.0 + jnp.tanh(GELU_COEF * (value + 0.044715 * value * value * value)))


def gelu_slope(value):
    inner = jnp.tanh(GELU_COEF * (value + 0.044715 * value * value * value))
    return 0.5 * (1.0 + inner) + 0.5 * value * (1.0 - inner * inner) * GELU_COEF * (
        1.0 + 3.0 * 0.044715 * value * value
    )


def adamw(weight, first, second, grad, rate, decay):
    first = BETA_ONE * first + (1.0 - BETA_ONE) * grad
    second = BETA_TWO * second + (1.0 - BETA_TWO) * grad * grad
    update = first / (1.0 - BETA_ONE**STEP) / (jnp.sqrt(second / (1.0 - BETA_TWO**STEP)) + ADAM_EPS)
    return (weight - rate * (update + decay * weight), first, second)


def local(
    tokens,
    cotangent,
    lengths,
    qkv_weight,
    qkv_first,
    qkv_second,
    dense_weight,
    dense_first,
    dense_second,
    up_weight,
    up_first,
    up_second,
    down_weight,
    down_first,
    down_second,
    qkv_bias,
    qkv_bias_first,
    qkv_bias_second,
    up_bias,
    up_bias_first,
    up_bias_second,
    vectors,
    vector_first,
    vector_second,
):
    xh, c = lax.axis_index("xh"), lax.axis_index("c")
    count, model = tokens.shape
    rows = 4 * count
    part = qkv_weight.shape[1]
    own_units = down_weight.shape[0]
    own_rows = dense_weight.shape[0]
    units = 16 * own_units
    heads = 256
    side = model // 2

    y, z = lax.axis_index("y"), lax.axis_index("z")
    place = jnp.stack([y, z]).astype(jnp.int32)
    cut = call(
        cut_columns, (1,),
        [full(*qkv_weight.shape), full(*up_weight.shape)],
        full(4, part, 3 * heads + units), struct((4, part, 3 * heads + units), LOW), (qkv_weight, up_weight),
    )
    cut = lax.all_to_all(cut, ("xh", "c"), 0, 0, tiled=True)
    dense_lines = dense_weight.astype(LOW).reshape(own_rows, 8, 256).transpose(1, 0, 2).reshape(2, 4 * own_rows, 256)
    down_low = down_weight.astype(LOW)
    q = cut[:, :, : 3 * heads]
    u = cut[:, :, 3 * heads :]
    payload = jnp.concatenate(
        [jnp.concatenate([q.reshape(4 * part, -1), dense_lines.reshape(4 * part, 256)], axis=1), u.reshape(4 * part, -1)]
        + [down_low[:, :side], down_low[:, side:]]
    )
    everything = lax.all_gather(payload, ("y", "z"), axis=0, tiled=False)

    n_vec = 4 * vectors.shape[1]
    n_bias = 3 * qkv_bias.shape[1]
    n_small = n_vec + n_bias + own_units
    small = [vectors.reshape(-1), qkv_bias.reshape(-1), up_bias, lengths[0].astype(WIDE)]
    small = jnp.concatenate(small).astype(LOW)
    small = jnp.pad(small, (0, 256 - small.shape[0]))
    small = jnp.broadcast_to(small[None, None], (64, 1, 256))
    payload, tokens_sent, small, cotangent, lengths = held(payload, tokens, small, cotangent, lengths)
    own_start, own_valid = starts(lengths[0], count)
    valid = own_valid[:, None].astype(WIDE)
    back_own = (cotangent.astype(WIDE) * valid).astype(LOW)

    small = lax.all_to_all(small, ("y", "xh", "z", "c"), 0, 0, tiled=True)

    tokens_near = across(tokens_sent)
    small, tokens_near = held(small, tokens_near)
    tokens_pair = jnp.stack([tokens, tokens_near])
    tokens_other = swap(tokens_pair, "c")
    tokens_other, back_own = held(tokens_other, back_own)
    back_near = across(back_own)
    back_pair = jnp.stack([back_own, back_near])
    back_other = swap(back_pair, "c")
    all_back = jnp.concatenate([back_pair, back_other]).reshape(rows, model)

    small = small.reshape(4, 2, 4, 2, 256).astype(WIDE)
    gains = small[..., :n_vec].reshape(64, 4, -1).transpose(1, 0, 2).reshape(4, model)
    in_chip = pick(small, xh, 1)
    b_qkv = in_chip[..., n_vec : n_vec + n_bias].reshape(2, 2, 4, 2, 3, -1)
    b_qkv = pick(b_qkv, c).transpose(3, 0, 1, 2, 4).reshape(1, 3 * heads)
    b_up = pick(in_chip, c, 2)[..., n_vec + n_bias : n_small].reshape(1, units)
    near = pick(pick(small, y), z, 1)[..., n_small : n_small + 4]
    order = [(xh, c), (1 - xh, c), (xh, 1 - c), (1 - xh, 1 - c)]
    all_lengths = jnp.stack([pick(pick(near, i), j) for i, j in order]).astype(jnp.int32)
    start, _ = jax.vmap(functools.partial(starts, count=count))(all_lengths)
    position = (jnp.arange(count, dtype=jnp.int32)[None, :] - start).reshape(-1, 1)
    start = start.reshape(-1, 1)
    half = ROT_DIMS // 2
    lane = jnp.arange(128, dtype=jnp.int32) % HEAD_DIM
    freq = 10000.0 ** (-2.0 * (lane % half).astype(WIDE) / (2 * half))
    angle = position.astype(WIDE) * freq[None, :]
    turned = (lane < ROT_DIMS)[None, :]
    cosine = jnp.where(turned, jnp.cos(angle), 1.0)
    sine = jnp.where(turned, jnp.sin(angle), 0.0)
    normed, scaled, turned_rows = call(
        norm_rows, (4,),
        [
            pl.BlockSpec((1, count, model), lambda i: (jnp.minimum(i, 1), 0, 0)),
            pl.BlockSpec((1, count, model), lambda i: (jnp.maximum(i - 2, 0), 0, 0)),
            full(4, model),
        ],
        [pl.BlockSpec((count, model), lambda i: (i, 0))] * 2 + [pl.BlockSpec((model, count), lambda i: (0, i))],
        [struct((rows, model), LOW)] * 2 + [struct((model, rows), LOW)],
        (tokens_pair, tokens_other, gains),
        8 * MICROSECOND,
    )
    everything, normed, scaled, turned_rows, cosine, sine, start, b_qkv, b_up, all_back = held(
        everything, normed, scaled, turned_rows, cosine, sine, start, b_qkv, b_up, all_back
    )

    def columns(n_rows):
        return pl.BlockSpec((n_rows, 256), lambda n: (0, n))

    whole = pl.BlockSpec(memory_space=pltpu.VMEM)
    active, d_hidden, g_feed, grad_up_bias = call(
        feed_forward, (4,),
        [
            whole, whole, whole,
            pl.BlockSpec((16, 4 * part, 256), lambda j: (0, 1, j)),
            pl.BlockSpec((4, 2 * part, side), lambda j: (j, 4, 0)),
            pl.BlockSpec((4, 2 * part, side), lambda j: (j, 5, 0)),
            columns(1),
        ],
        [columns(rows), columns(rows), whole, columns(1)],
        [struct((rows, units), LOW)] * 2 + [struct((16, 8 * part, side), LOW), struct((1, units), WIDE)],
        (normed, turned_rows, all_back, everything, everything, everything, b_up),
        29 * MICROSECOND, 56,
    )
    g_feed, normed, all_back = held(g_feed, normed, all_back)

    late = lax.psum_scatter(g_feed.reshape(-1, side), ("y", "z"), scatter_dimension=0, tiled=True)
    lines = everything[:, : 4 * part, 3 * heads :].reshape(2, 2, 4, 2, 4, own_rows, 256)
    other = swap(pick(lines, 1 - c), "c")
    lines = by_source(c, pick(lines, c), other, 2)
    dense = lines.transpose(3, 4, 0, 1, 2, 5, 6).reshape(8, heads, 256)
    joined, d_mixed = call(
        project, (3,),
        [whole, whole, pl.BlockSpec((16, 4 * part, heads), lambda w: (0, 0, w)), whole],
        [columns(rows), whole],
        [struct((rows, 3 * heads), WIDE), struct((rows, heads), LOW)],
        (normed, all_back, everything, dense),
        9 * MICROSECOND,
    )
    mixed, d_joined = attention(joined, b_qkv, d_mixed, start, cosine, sine, count)

    def pair_sum(keep, got):
        return [wide_sum(keep[i * count : (i + 1) * count], got[i * count : (i + 1) * count]).astype(LOW) for i in range(2)]

    halves = [struct((2 * count, model), LOW)] * 2
    d_keep, d_send, gv_part = call(
        normed_parts, (8,),
        [
            whole, whole, columns(rows),
            pl.BlockSpec((2, 4 * part, side), lambda n: (n, 0, 0)),
            pl.BlockSpec((2, 4 * part, side), lambda n: (n, 1, 0)),
        ],
        [columns(2 * count)] * 2 + [columns(2)],
        halves + [struct((2, model), WIDE)],
        (d_joined, d_hidden, scaled, everything, everything),
        13 * MICROSECOND,
    )
    d_keep, d_send, mixed, d_joined = held(d_keep, d_send, mixed, d_joined)

    d_pair = pair_sum(d_keep, swap(d_send, "c"))
    d_pair[0], d_pair[1], mixed, d_joined = held(*d_pair, mixed, d_joined)
    d_near = across(d_pair[1])
    b_keep, b_send = call(
        branch_parts, (8,),
        [
            whole, whole, pl.BlockSpec((1, heads, 256), lambda n: (n, 0, 0)),
            pl.BlockSpec((16, 2 * part, 256), lambda n: (0, 4 + n // 4, n % 4)),
        ],
        [columns(2 * count)] * 2, halves,
        (mixed, active, dense, everything),
        1,
    )
    strip = pl.BlockSpec((1, heads, 256), lambda n, s: (n, 0, 0))
    grad_qkv, g_dense, grad_qkv_bias = call_at(
        attention_grads, place, (8,),
        [pl.BlockSpec((256, rows), lambda n, s: (n, 0)), whole, whole, pl.BlockSpec((rows, 256), lambda n, s: (0, n))],
        [whole, strip, whole],
        [struct((4, 2, 8 * part, 3 * heads), LOW), struct((8, heads, 256), LOW), struct((1, 3 * heads), WIDE)],
        (turned_rows, d_joined, mixed, all_back),
        1,
    )
    d_near, b_keep, b_send, grad_qkv, g_dense, grad_qkv_bias = held(
        d_near, b_keep, b_send, grad_qkv, g_dense, grad_qkv_bias
    )

    d_own = wide_sum(d_pair[0], d_near).astype(LOW)
    d_last = swap(d_own, "mp")
    g_dense = g_dense.reshape(2, 4, 2, 4, 2, own_rows, 256)
    other = swap(pick(g_dense, 1 - c, 4), "c")
    b_pair = pair_sum(b_keep, swap(b_send, "c"))
    g_dense = by_source(c, pick(g_dense, c, 4), other, 2)
    g_dense = g_dense.transpose(2, 3, 4, 0, 1, 5, 6).reshape(4, 2, 8 * part, 256)
    grads = jnp.concatenate([grad_qkv, jnp.roll(g_dense, -y, 0)], axis=3)
    grads, b_pair[0], b_pair[1] = held(grads, *b_pair)

    hops = scatter_first(grads, "y")
    b_near = across(b_pair[1])
    column_sum = jnp.sum(cotangent.astype(WIDE) * valid, axis=0)
    column_sum = 0.5 * column_sum.reshape(4, 2, 4, 2, part)
    gv = gv_part.reshape(2, 4, 4, 2, 2, part).transpose(1, 3, 2, 4, 0, 5)
    gv = jnp.concatenate([gv.reshape(4, 2, 4, 2, 2 * part), column_sum], axis=4)
    gb = grad_qkv_bias.reshape(3, 2, 4, 2, -1).transpose(1, 2, 3, 0, 4).reshape(2, 1, 4, 2, n_bias)
    gb = lax.dynamic_update_slice(jnp.zeros((4, 2, 4, 2, n_bias), WIDE), gb, (2 * c, xh, 0, 0, 0))
    gu = grad_up_bias.reshape(4, 1, 4, 1, own_units)
    gu = lax.dynamic_update_slice(jnp.zeros((4, 2, 4, 2, own_units), WIDE), gu, (0, xh, 0, c, 0))
    n_v = 3 * part
    pack = jnp.concatenate([gv, gb, gu], axis=4).reshape(64, 1, n_v + n_bias + own_units)
    pack = jnp.pad(pack, ((0, 0), (0, 0), (0, 256 - pack.shape[2])))
    pack = lax.all_to_all(pack, ("y", "xh", "z", "c"), 0, 0, tiled=True)
    pack = jnp.sum(pack, axis=0)
    hops, b_near, d_last, pack, late = held(hops, b_near, d_last, pack, late)
    last = scatter_last(grads, hops, "y")
    b_own = wide_sum(b_pair[0], b_near).astype(LOW)
    b_last = swap(b_own, "mp")
    own_up = lax.all_to_all(late[: 4 * part].reshape(4, part, units), ("xh", "c"), 0, 0, tiled=True)
    last = held(*last)
    early = scatter_direct(scatter_join(grads, hops, last).reshape(4, 4 * part, side), "z")
    vector_sum = pack[0, :n_v]
    vector_sum = vector_sum + swap(vector_sum, "mp")

    own_qkv = lax.all_to_all(early[:, : 3 * heads].astype(LOW).reshape(4, part, 3 * heads), ("xh", "c"), 0, 0, tiled=True)
    owned_down = jnp.concatenate([late[4 * part : 6 * part], late[6 * part :]], axis=1).astype(WIDE)
    owned_dense = early[:, 3 * heads :].reshape(8, own_rows, 256).transpose(1, 0, 2).reshape(own_rows, model)
    got_vectors = vector_sum.reshape(3, part)
    owned_vectors = jnp.concatenate([got_vectors, got_vectors[2:]])
    owned_qkv_bias = pack[0, n_v : n_v + n_bias].reshape(qkv_bias.shape)
    owned_up_bias = pack[0, n_v + n_bias : n_v + n_bias + own_units]

    output = (tokens.astype(WIDE) + wide_sum(b_own, b_last) + gains[2] + gains[3]).astype(LOW)

    def half_rows(n):
        return pl.BlockSpec((count // 2, n), lambda i: (i, 0))

    input_grad = call(
        input_rows, (2,),
        [half_rows(model), half_rows(model), half_rows(1), half_rows(model), half_rows(model), full(4, model)],
        half_rows(model), struct((count, model), WIDE),
        (tokens, cotangent, valid, d_own, d_last, gains),
    )
    mine = (qkv_weight, qkv_first, qkv_second)
    new_qkv = call(
        update_qkv, (1,),
        [full(4, part, 3 * heads)] + [full(*x.shape) for x in mine],
        [full(*x.shape) for x in mine], [struct(x.shape, WIDE) for x in mine], (own_qkv,) + mine,
    )
    mine = (up_weight, up_first, up_second)
    new_up = call(
        update_up, (1,),
        [full(4, part, units)] + [full(*x.shape) for x in mine],
        [full(*x.shape) for x in mine], [struct(x.shape, WIDE) for x in mine], (own_up,) + mine,
    )
    new_dense = adamw(dense_weight, dense_first, dense_second, owned_dense, 0.2, WEIGHT_DECAY)
    new_down = adamw(down_weight, down_first, down_second, owned_down, 0.03, WEIGHT_DECAY)
    new_qkv_bias = adamw(qkv_bias, qkv_bias_first, qkv_bias_second, owned_qkv_bias, 0.5, 0.0)
    new_up_bias = adamw(up_bias, up_bias_first, up_bias_second, owned_up_bias, 0.5, 0.0)
    new_vectors = adamw(vectors, vector_first, vector_second, owned_vectors, 0.5, 0.0)
    return (output, input_grad, *new_qkv, *new_dense, *new_up, *new_down, *new_qkv_bias, *new_up_bias, *new_vectors)


def solution(mesh):
    mesh = Mesh(mesh.devices.reshape(4, 2, 4, 2, 2), ("y", "xh", "z", "c", "mp"))
    dp = ("y", "xh", "z", "c")
    both = ("mp",) + dp
    weights = (P(None, dp, "mp"),) * 3 + (P(both, None),) * 3 + (P(dp, "mp"),) * 3 + (P(both, None),) * 3
    smalls = (P(None, both),) * 3 + (P(both),) * 3 + (P(None, dp),) * 3
    rows = P(dp, None)
    in_specs = (rows, rows, rows) + weights + smalls
    out_specs = (rows, rows) + weights + smalls
    return jax.shard_map(local, mesh=mesh, in_specs=in_specs, out_specs=out_specs, check_vma=False)
```

```python
import functools
import math

import jax
import jax.numpy as jnp
from jax import lax
from jax.experimental import pallas as pl
from jax.experimental.pallas import tpu as pltpu
from jax.sharding import Mesh, PartitionSpec as P

HEAD_DIM = 64
ROT_DIMS = 32
STEP = 10


BETA_ONE = 0.9
BETA_TWO = 0.95
ADAM_EPS = 1e-08
WEIGHT_DECAY = 0.1
NORM_EPS = 1e-05
MASKED = -1e30
GELU_COEF = 0.7978845608028654

LOW = jnp.bfloat16
WIDE = jnp.float32
RING = 4
MICROSECOND = 1100000000


def shift(x, axis, step):
    size = lax.axis_size(axis)
    return lax.ppermute(x, axis, [(i, (i + step) % size) for i in range(size)])


def swap(x, axis):
    return shift(x, axis, 1)


def across(x):
    return lax.ppermute(x, ("xh", "mp"), [(0, 3), (3, 0), (1, 2), (2, 1)])


def by_source(index, own, other, dim=0):
    low = jnp.where(index == 0, own, other)
    high = jnp.where(index == 0, other, own)
    return jnp.stack([low, high], axis=dim)


def pick(x, index, dim=0):
    return lax.dynamic_index_in_dim(x, index, dim, keepdims=False)


def wide_sum(*xs):
    return functools.reduce(lambda a, b: a + b, [x.astype(WIDE) for x in xs])


def scatter_direct(x, axis):
    me = lax.axis_index(axis)
    own, right, far, left = [pick(x, lax.rem(me + k, RING)) for k in range(RING)]
    return wide_sum(own, shift(right, axis, 1), shift(left, axis, -1), shift(far, axis, 2))


def scatter_first(x, axis):
    flat = x.reshape((2 * RING,) + x.shape[2:])
    return shift(flat[3:5], axis, 1), shift(flat[5:7], axis, -1)


def scatter_last(x, got, axis):
    from_left, from_right = got
    on_right = wide_sum(x[1, 0], from_left[1]).astype(LOW)
    on_left = wide_sum(x[3, 1], from_right[0]).astype(LOW)
    return shift(on_right, axis, 1), shift(on_left, axis, -1)


def scatter_join(x, got, last, kind=LOW):
    from_left, from_right = got
    top = wide_sum(x[0, 0], from_right[1], last[0])
    bottom = wide_sum(x[0, 1], from_left[0], last[1])
    return jnp.stack([top, bottom]).astype(kind)


def dot(a, b, da, db):
    return lax.dot_general(a, b, (((da,), (db,)), ((), ())), preferred_element_type=WIDE)


def call(kernel, grid, in_specs, out_specs, out_shape, args, flops=0, limit=48, scratch=(), aliases=None):
    moved = sum(a.size * a.dtype.itemsize for a in args) if flops > 1 else 1
    return pl.pallas_call(
        kernel,
        grid=grid,
        in_specs=in_specs,
        out_specs=out_specs,
        out_shape=out_shape,
        scratch_shapes=scratch,
        input_output_aliases=aliases or {},
        compiler_params=pltpu.CompilerParams(vmem_limit_bytes=limit * 1024 * 1024),
        cost_estimate=pl.CostEstimate(flops=flops, bytes_accessed=moved, transcendentals=0),
    )(*args)


def struct(shape, dtype):
    return jax.ShapeDtypeStruct(shape, dtype)


def full(*shape):
    return pl.BlockSpec(shape, lambda *i: (0,) * len(shape))


PLACES = [((y * 2 + xh) * 4 + z, (y * 4 + z) * 2 + xh) for y in range(4) for xh in range(2) for z in range(4)]
HERE = [here for here, _ in sorted(PLACES, key=lambda p: p[1])]
THERE = [there for _, there in sorted(PLACES)]


def reorder(x, order):
    return jnp.concatenate([x[:, 64 * k : 64 * (k + 1)] for k in order], axis=1)


def cut_columns(qkv_ref, up_ref, out_ref):
    for xh in range(2):
        for c in range(2):
            to = xh * 2 + c
            for w in range(3):
                for low in range(2):
                    at = (2 * c + low) * 256 + xh * 128
                    out_ref[to, :, w * 256 + low * 128 : w * 256 + (low + 1) * 128] = qkv_ref[w, :, at : at + 128].astype(LOW)
            for pair in range(8):
                y, z = pair // 2, 2 * (pair % 2)
                at = y * 1024 + xh * 512 + z * 128 + c * 64
                piece = jnp.concatenate([up_ref[:, at : at + 64], up_ref[:, at + 128 : at + 192]], axis=1)
                out_ref[to, :, 768 + pair * 128 : 768 + (pair + 1) * 128] = piece.astype(LOW)


def normalise(x):
    centered = x - jnp.mean(x, axis=-1, keepdims=True)
    inverse = lax.rsqrt(jnp.mean(centered * centered, axis=-1, keepdims=True) + NORM_EPS)
    return centered * inverse, inverse


def norm_rows(pair_ref, other_ref, gains_ref, normed_ref, scaled_ref, turned_ref):
    def run(ref):
        scaled, _ = normalise(ref[0].astype(WIDE))
        normed = reorder(scaled * gains_ref[0:1] + gains_ref[1:2], HERE)
        normed_ref[...] = normed.astype(LOW)
        scaled_ref[...] = reorder(scaled, HERE).astype(LOW)
        for k in range(8):
            turned_ref[k * 256 : (k + 1) * 256, :] = normed[:, k * 256 : (k + 1) * 256].T.astype(LOW)

    pl.when(pl.program_id(0) < 2)(lambda: run(pair_ref))
    pl.when(pl.program_id(0) >= 2)(lambda: run(other_ref))


def attention_grads(turned_ref, d_joined_ref, others, out_ref):
    width = d_joined_ref.shape[1]
    grad = dot(turned_ref[...], d_joined_ref[...], 1, 0).astype(LOW)
    blocks, size = out_ref.shape[:2]
    for k in range(blocks):
        out_ref[k, :, :width] = grad[k * size : (k + 1) * size]
        out_ref[k, :, width:] = jnp.zeros((size, out_ref.shape[2] - width), LOW)


def feed_forward(
    normed_ref, turned_ref, back_ref, up_ref, down_a_ref, down_b_ref, bias_ref,
    active_ref, d_hidden_ref, d_bias_ref, grads_out, up_ref_out, down_ref_out, sems,
):
    step, steps = pl.program_id(0), pl.num_programs(0)
    model = normed_ref.shape[1]
    half = model // 2
    width = active_ref.shape[1]
    slot = lax.rem(step, 2)

    def stores(slot, at):
        column = pl.multiple_of(at * width, width)
        return [
            pltpu.make_async_copy(
                up_ref_out.at[slot], grads_out.at[:, pl.ds(128, 128), pl.ds(column, width)], sems.at[slot, 0]
            ),
            pltpu.make_async_copy(
                down_ref_out.at[slot], grads_out.at[pl.ds(at * 4, 4), pl.ds(256, 128), :], sems.at[slot, 1]
            ),
        ]

    hidden = dot(normed_ref[...], up_ref[...].reshape(model, width), 1, 0) + bias_ref[...]
    down = jnp.concatenate([down_a_ref[...].reshape(width, half), down_b_ref[...].reshape(width, half)], axis=1)
    d_active = dot(back_ref[...], down, 1, 1)
    square = hidden * hidden
    inner = jnp.tanh(GELU_COEF * (hidden + 0.044715 * square * hidden))
    ends = 0.5 * (1.0 + inner)
    active = (hidden * ends).astype(LOW)
    slope = ends + 0.5 * hidden * (1.0 - inner * inner) * GELU_COEF * (1.0 + 3.0 * 0.044715 * square)
    d_hidden = (d_active * slope).astype(LOW)
    active_ref[...] = active
    d_hidden_ref[...] = d_hidden
    d_bias_ref[...] = jnp.sum(d_hidden.astype(WIDE), axis=0, keepdims=True)

    @pl.when(step >= 2)
    def _():
        for x in stores(slot, step - 2):
            x.wait()

    up_grad = dot(turned_ref[...], d_hidden, 1, 0).astype(LOW)
    down_grad = dot(active, back_ref[...], 0, 0).astype(LOW)
    for k in range(16):
        up_ref_out[slot, k] = up_grad[k * 128 : (k + 1) * 128]
    for z in range(4):
        down_ref_out[slot, z, :64] = down_grad[z * 64 : (z + 1) * 64, :half]
        down_ref_out[slot, z, 64:] = down_grad[z * 64 : (z + 1) * 64, half:]
    for x in stores(slot, step):
        x.start()

    @pl.when(step == steps - 1)
    def _():
        for x in stores(1 - slot, step - 1):
            x.wait()
        for x in stores(slot, step):
            x.wait()


def branch_parts(mixed_ref, active_ref, dense_ref, down_ref, keep_ref, send_ref):
    branch = dot(mixed_ref[...], dense_ref[0], 1, 0)
    branch += dot(active_ref[...], down_ref[...].reshape(active_ref.shape[1], -1), 1, 0)
    branch = branch.astype(LOW)
    half = branch.shape[0] // 2
    keep_ref[...] = branch[:half]
    send_ref[...] = branch[half:]


def normed_parts(d_joined_ref, d_hidden_ref, scaled_ref, qkv_ref, up_ref, keep_ref, send_ref, sums_ref):
    half, width = keep_ref.shape
    total = dot(d_joined_ref[...], qkv_ref[...].reshape(width, -1)[:, : d_joined_ref.shape[1]], 1, 1)
    total += dot(d_hidden_ref[...], up_ref[...].reshape(width, -1), 1, 1)
    low = total.astype(LOW)
    keep_ref[...] = low[:half]
    send_ref[...] = low[half:]
    sums_ref[0:1] = jnp.sum(total * scaled_ref[...].astype(WIDE), axis=0, keepdims=True)
    sums_ref[1:2] = jnp.sum(total, axis=0, keepdims=True)


def input_rows(tokens_ref, cotangent_ref, valid_ref, d_one_ref, d_two_ref, gains_ref, grad_ref):
    scaled, inverse = normalise(tokens_ref[...].astype(WIDE))
    upstream = cotangent_ref[...].astype(WIDE) * valid_ref[...]
    d_normed = reorder(d_one_ref[...].astype(WIDE) + d_two_ref[...].astype(WIDE), THERE)
    d_scaled = d_normed * gains_ref[0:1]
    grad_ref[...] = upstream + inverse * (
        d_scaled
        - jnp.mean(d_scaled, axis=-1, keepdims=True)
        - scaled * jnp.mean(d_scaled * scaled, axis=-1, keepdims=True)
    )


def update_qkv(grad_ref, weight_ref, first_ref, second_ref, *out_refs):
    for xh in range(2):
        for y in range(4):
            for w in range(3):
                at = slice(y * 256 + xh * 128, y * 256 + (xh + 1) * 128)
                here = w * 256 + (y % 2) * 128
                grad = grad_ref[xh * 2 + y // 2, :, here : here + 128].astype(WIDE)
                new = adamw(weight_ref[w, :, at], first_ref[w, :, at], second_ref[w, :, at], grad, 0.05, WEIGHT_DECAY)
                for ref, value in zip(out_refs, new):
                    ref[w, :, at] = value


def update_up(grad_ref, weight_ref, first_ref, second_ref, *out_refs):
    for xh in range(2):
        for y in range(4):
            for z in range(4):
                base = y * 1024 + xh * 512 + z * 128
                at = slice(base, base + 128)
                here = 768 + (y * 4 + z) * 64
                grad = jnp.concatenate(
                    [grad_ref[xh * 2 + c, :, here : here + 64].astype(WIDE) for c in range(2)], axis=1
                )
                new = adamw(weight_ref[:, at], first_ref[:, at], second_ref[:, at], grad, 0.05, WEIGHT_DECAY)
                for ref, value in zip(out_refs, new):
                    ref[:, at] = value


def held(*xs):
    return lax.optimization_barrier(xs)


def attend(
    normed_ref, weight_ref, bias_ref, back_ref, dense_ref, start_ref, cos_ref, sin_ref,
    mixed_ref, d_joined_ref, g_dense_ref, d_bias_ref, joined_ref, sum_ref,
):
    count, width = mixed_ref.shape
    weight = weight_ref[...].reshape(normed_ref.shape[1], -1)
    joined_ref[...] = lax.dot_general(normed_ref[...], weight, (((1,), (0,)), ((), ())), preferred_element_type=WIDE)
    back = back_ref[...]
    pieces = dense_ref.shape[0]
    dense = jnp.concatenate([dense_ref[k] for k in range(pieces)], axis=1)
    d_mixed = lax.dot_general(back, dense, (((1,), (1,)), ((), ())), preferred_element_type=WIDE).astype(LOW)
    heads = width // HEAD_DIM
    lanes = 128
    lane = lax.broadcasted_iota(jnp.int32, (count, lanes), 1) % HEAD_DIM
    cosine = cos_ref[...]
    sine = sin_ref[...]
    half = ROT_DIMS // 2
    low_sine = jnp.where(lane < half, sine, 0.0)
    high_sine = jnp.where((lane >= half) & (lane < ROT_DIMS), sine, 0.0)

    def turn(x, sign):
        up = pltpu.roll(x, half, 1) * high_sine
        down = pltpu.roll(x, lanes - half, 1) * low_sine
        return x * cosine + sign * (up - down)

    place = lax.broadcasted_iota(jnp.int32, (count, count), 0)
    other = lax.broadcasted_iota(jnp.int32, (count, count), 1)
    allowed = (other >= start_ref[...]) & (other <= place)
    scale = HEAD_DIM ** (-0.5)

    def dot(a, b, da, db):
        return lax.dot_general(a, b, (((da,), (db,)), ((), ())), preferred_element_type=WIDE)

    for pair in range(width // lanes):
        at = pair * lanes
        query2 = turn(joined_ref[:, at : at + lanes] + bias_ref[:, at : at + lanes], 1.0).astype(LOW)
        k_at = width + at
        keys2 = turn(joined_ref[:, k_at : k_at + lanes] + bias_ref[:, k_at : k_at + lanes], 1.0).astype(LOW)
        v_at = 2 * width + at
        values2 = (joined_ref[:, v_at : v_at + lanes] + bias_ref[:, v_at : v_at + lanes]).astype(LOW)
        d_out2 = d_mixed[:, at : at + lanes]
        mixed, d_query, d_keys, d_values = [], [], [], []
        for h in range(lanes // HEAD_DIM):
            cut = slice(h * HEAD_DIM, (h + 1) * HEAD_DIM)
            query, keys, values, d_out = query2[:, cut], keys2[:, cut], values2[:, cut], d_out2[:, cut]
            scores = jnp.where(allowed, dot(query, keys, 1, 1) * scale, MASKED)
            expo = jnp.exp(scores - jnp.max(scores, axis=1, keepdims=True))
            weights = expo / jnp.sum(expo, axis=1, keepdims=True)
            weights_low = weights.astype(LOW)
            mixed.append(dot(weights_low, values, 1, 0))
            d_weights = dot(d_out, values, 1, 1)
            d_values.append(dot(weights_low, d_out, 0, 0))
            delta = jnp.sum(weights * d_weights, axis=1, keepdims=True)
            d_scores = (weights * (d_weights - delta)).astype(LOW)
            d_query.append(dot(d_scores, keys, 1, 0) * scale)
            d_keys.append(dot(d_scores, query, 0, 0) * scale)
        mixed_ref[:, at : at + lanes] = jnp.concatenate(mixed, axis=1).astype(LOW)
        d_joined_ref[:, at : at + lanes] = turn(jnp.concatenate(d_query, axis=1), -1.0).astype(LOW)
        d_joined_ref[:, k_at : k_at + lanes] = turn(jnp.concatenate(d_keys, axis=1), -1.0).astype(LOW)
        d_joined_ref[:, v_at : v_at + lanes] = jnp.concatenate(d_values, axis=1).astype(LOW)

    step = pl.program_id(0)

    @pl.when(step == 0)
    def _():
        sum_ref[...] = jnp.zeros_like(sum_ref)
        d_bias_ref[...] = jnp.zeros_like(d_bias_ref)

    sum_ref[...] += dot(mixed_ref[...], back, 0, 0)
    d_bias_ref[...] += jnp.sum(d_joined_ref[...].astype(WIDE), axis=0, keepdims=True)

    @pl.when(step == pl.num_programs(0) - 1)
    def _():
        size = back.shape[1] // pieces
        for k in range(pieces):
            g_dense_ref[k] = sum_ref[:, k * size : (k + 1) * size].astype(LOW)


def attention(normed, weights, bias, back, dense, start, cosine, sine, count):
    rows, model = back.shape
    width = dense.shape[1]

    def block(columns):
        return pl.BlockSpec((count, columns), lambda r: (r, 0))

    return pl.pallas_call(
        attend,
        grid=(rows // count,),
        in_specs=[
            block(model),
            pl.BlockSpec((16, model // 16, 3 * width), lambda r: (0, 0, 0)),
            pl.BlockSpec((1, 3 * width), lambda r: (0, 0)),
            block(model),
            pl.BlockSpec(dense.shape, lambda r: (0, 0, 0)),
            block(1),
            block(128),
            block(128),
        ],
        out_specs=[
            block(width),
            block(3 * width),
            pl.BlockSpec(dense.shape, lambda r: (0, 0, 0)),
            pl.BlockSpec((1, 3 * width), lambda r: (0, 0)),
        ],
        out_shape=[
            jax.ShapeDtypeStruct((rows, width), LOW),
            jax.ShapeDtypeStruct((rows, 3 * width), LOW),
            jax.ShapeDtypeStruct(dense.shape, LOW),
            jax.ShapeDtypeStruct((1, 3 * width), WIDE),
        ],
        scratch_shapes=[pltpu.VMEM((count, 3 * width), WIDE), pltpu.VMEM((width, model), WIDE)],
        compiler_params=pltpu.CompilerParams(vmem_limit_bytes=56 * 1024 * 1024),
        cost_estimate=pl.CostEstimate(flops=18 * MICROSECOND, bytes_accessed=rows * model * 2, transcendentals=0),
    )(normed, weights, bias, back, dense, start, cosine, sine)


def starts(lengths_row, count):
    finish = jnp.cumsum(lengths_row)
    place = jnp.arange(count, dtype=jnp.int32)
    passed = place[:, None] >= finish[None, :]
    start = jnp.max(jnp.where(passed, finish[None, :], 0), axis=1)
    return start, place < finish[-1]


def gelu(value):
    return 0.5 * value * (1.0 + jnp.tanh(GELU_COEF * (value + 0.044715 * value * value * value)))


def gelu_slope(value):
    inner = jnp.tanh(GELU_COEF * (value + 0.044715 * value * value * value))
    return 0.5 * (1.0 + inner) + 0.5 * value * (1.0 - inner * inner) * GELU_COEF * (
        1.0 + 3.0 * 0.044715 * value * value
    )


def adamw(weight, first, second, grad, rate, decay):
    first = BETA_ONE * first + (1.0 - BETA_ONE) * grad
    second = BETA_TWO * second + (1.0 - BETA_TWO) * grad * grad
    update = first / (1.0 - BETA_ONE**STEP) / (jnp.sqrt(second / (1.0 - BETA_TWO**STEP)) + ADAM_EPS)
    return (weight - rate * (update + decay * weight), first, second)


def local(
    tokens,
    cotangent,
    lengths,
    qkv_weight,
    qkv_first,
    qkv_second,
    dense_weight,
    dense_first,
    dense_second,
    up_weight,
    up_first,
    up_second,
    down_weight,
    down_first,
    down_second,
    qkv_bias,
    qkv_bias_first,
    qkv_bias_second,
    up_bias,
    up_bias_first,
    up_bias_second,
    vectors,
    vector_first,
    vector_second,
):
    xh, c = lax.axis_index("xh"), lax.axis_index("c")
    count, model = tokens.shape
    rows = 4 * count
    part = qkv_weight.shape[1]
    own_units = down_weight.shape[0]
    own_rows = dense_weight.shape[0]
    units = 16 * own_units
    heads = 256
    side = model // 2

    y, z = lax.axis_index("y"), lax.axis_index("z")
    cut = call(
        cut_columns, (1,),
        [full(*qkv_weight.shape), full(*up_weight.shape)],
        full(4, part, 3 * heads + units), struct((4, part, 3 * heads + units), LOW), (qkv_weight, up_weight),
    )
    cut = lax.all_to_all(cut, ("xh", "c"), 0, 0, tiled=True)
    dense_lines = dense_weight.astype(LOW).reshape(own_rows, 8, 256).transpose(1, 0, 2).reshape(2, 4 * own_rows, 256)
    down_low = down_weight.astype(LOW)
    q = cut[:, :, : 3 * heads]
    u = cut[:, :, 3 * heads :]
    payload = jnp.concatenate(
        [jnp.concatenate([q.reshape(4 * part, -1), dense_lines.reshape(4 * part, 256)], axis=1), u.reshape(4 * part, -1)]
        + [down_low[:, :side], down_low[:, side:]]
    )
    everything = lax.all_gather(payload, ("y", "z"), axis=0, tiled=False)

    n_vec = 4 * vectors.shape[1]
    n_bias = 3 * qkv_bias.shape[1]
    n_small = n_vec + n_bias + own_units
    small = [vectors.reshape(-1), qkv_bias.reshape(-1), up_bias, lengths[0].astype(WIDE)]
    small = jnp.concatenate(small).astype(LOW)
    small = jnp.pad(small, (0, 256 - small.shape[0]))
    small = jnp.broadcast_to(small[None, None], (64, 1, 256))
    payload, tokens_sent, small, cotangent, lengths = held(payload, tokens, small, cotangent, lengths)
    own_start, own_valid = starts(lengths[0], count)
    valid = own_valid[:, None].astype(WIDE)
    back_own = (cotangent.astype(WIDE) * valid).astype(LOW)

    small = lax.all_to_all(small, ("y", "xh", "z", "c"), 0, 0, tiled=True)

    tokens_near = across(tokens_sent)
    small, tokens_near = held(small, tokens_near)
    tokens_pair = jnp.stack([tokens, tokens_near])
    tokens_other = swap(tokens_pair, "c")
    tokens_other, back_own = held(tokens_other, back_own)
    back_near = across(back_own)
    back_pair = jnp.stack([back_own, back_near])
    back_other = swap(back_pair, "c")
    all_back = jnp.concatenate([back_pair, back_other]).reshape(rows, model)

    small = small.reshape(4, 2, 4, 2, 256).astype(WIDE)
    gains = small[..., :n_vec].reshape(64, 4, -1).transpose(1, 0, 2).reshape(4, model)
    in_chip = pick(small, xh, 1)
    b_qkv = in_chip[..., n_vec : n_vec + n_bias].reshape(2, 2, 4, 2, 3, -1)
    b_qkv = pick(b_qkv, c).transpose(3, 0, 1, 2, 4).reshape(1, 3 * heads)
    b_up = pick(in_chip, c, 2)[..., n_vec + n_bias : n_small].reshape(1, units)
    near = pick(pick(small, y), z, 1)[..., n_small : n_small + 4]
    order = [(xh, c), (1 - xh, c), (xh, 1 - c), (1 - xh, 1 - c)]
    all_lengths = jnp.stack([pick(pick(near, i), j) for i, j in order]).astype(jnp.int32)
    start, _ = jax.vmap(functools.partial(starts, count=count))(all_lengths)
    position = (jnp.arange(count, dtype=jnp.int32)[None, :] - start).reshape(-1, 1)
    start = start.reshape(-1, 1)
    half = ROT_DIMS // 2
    lane = jnp.arange(128, dtype=jnp.int32) % HEAD_DIM
    freq = 10000.0 ** (-2.0 * (lane % half).astype(WIDE) / (2 * half))
    angle = position.astype(WIDE) * freq[None, :]
    turned = (lane < ROT_DIMS)[None, :]
    cosine = jnp.where(turned, jnp.cos(angle), 1.0)
    sine = jnp.where(turned, jnp.sin(angle), 0.0)
    normed, scaled, turned_rows = call(
        norm_rows, (4,),
        [
            pl.BlockSpec((1, count, model), lambda i: (jnp.minimum(i, 1), 0, 0)),
            pl.BlockSpec((1, count, model), lambda i: (jnp.maximum(i - 2, 0), 0, 0)),
            full(4, model),
        ],
        [pl.BlockSpec((count, model), lambda i: (i, 0))] * 2 + [pl.BlockSpec((model, count), lambda i: (0, i))],
        [struct((rows, model), LOW)] * 2 + [struct((model, rows), LOW)],
        (tokens_pair, tokens_other, gains),
        8 * MICROSECOND,
    )
    everything, normed, scaled, turned_rows, cosine, sine, start, b_qkv, b_up, all_back = held(
        everything, normed, scaled, turned_rows, cosine, sine, start, b_qkv, b_up, all_back
    )

    def columns(n_rows):
        return pl.BlockSpec((n_rows, 256), lambda n: (0, n))

    whole = pl.BlockSpec(memory_space=pltpu.VMEM)
    anywhere = pl.BlockSpec(memory_space=pl.ANY)

    lines = everything[:, : 4 * part, 3 * heads :].reshape(2, 2, 4, 2, 4, own_rows, 256)
    other = swap(pick(lines, 1 - c), "c")
    active, d_hidden, grad_up_bias, grads = call(
        feed_forward, (4,),
        [
            whole, whole, whole,
            pl.BlockSpec((16, 4 * part, 256), lambda j: (0, 1, j)),
            pl.BlockSpec((4, 2 * part, side), lambda j: (j, 4, 0)),
            pl.BlockSpec((4, 2 * part, side), lambda j: (j, 5, 0)),
            columns(1),
        ],
        [columns(rows), columns(rows), columns(1), anywhere],
        [struct((rows, units), LOW)] * 2 + [struct((1, units), WIDE), struct((16, 12 * part, side), LOW)],
        (normed, turned_rows, all_back, everything, everything, everything, b_up),
        1, 56,
        [
            pltpu.VMEM((2, 16, 4 * part, 256), LOW),
            pltpu.VMEM((2, 4, 4 * part, side), LOW),
            pltpu.SemaphoreType.DMA((2, 2)),
        ],
    )
    active, d_hidden, grads, other, normed, all_back = held(active, d_hidden, grads, other, normed, all_back)
    lines = by_source(c, pick(lines, c), other, 2)
    dense = lines.transpose(3, 4, 0, 1, 2, 5, 6).reshape(8, heads, 256)
    mixed, d_joined, g_dense, grad_qkv_bias = attention(
        normed, everything, b_qkv, all_back, dense, start, cosine, sine, count
    )
    g_dense = g_dense.reshape(2, 4, 2, 4, 2, own_rows, 256)
    g_other = swap(pick(g_dense, 1 - c, 4), "c")
    grads = call(
        attention_grads, (4,),
        [pl.BlockSpec((512, rows), lambda n: (n, 0)), whole, anywhere],
        pl.BlockSpec((4, 4 * part, side), lambda n: (n, 0, 0)), struct((16, 12 * part, side), LOW),
        (turned_rows, d_joined, grads),
        1, 56, (), {2: 0},
    )
    grads, g_other, d_joined = held(grads, g_other, d_joined)

    late = lax.psum_scatter(grads.reshape(-1, side), ("y", "z"), scatter_dimension=0, tiled=True)

    def pair_sum(keep, got):
        return [wide_sum(keep[i * count : (i + 1) * count], got[i * count : (i + 1) * count]).astype(LOW) for i in range(2)]

    halves = [struct((2 * count, model), LOW)] * 2
    d_keep, d_send, gv_part = call(
        normed_parts, (8,),
        [
            whole, whole, columns(rows),
            pl.BlockSpec((2, 4 * part, side), lambda n: (n, 0, 0)),
            pl.BlockSpec((2, 4 * part, side), lambda n: (n, 1, 0)),
        ],
        [columns(2 * count)] * 2 + [columns(2)],
        halves + [struct((2, model), WIDE)],
        (d_joined, d_hidden, scaled, everything, everything),
        1,
    )
    d_keep, d_send, gv_part, mixed = held(d_keep, d_send, gv_part, mixed)

    d_pair = pair_sum(d_keep, swap(d_send, "c"))
    gv_other = swap(gv_part, "mp")
    d_pair[0], d_pair[1], gv_other, mixed = held(*d_pair, gv_other, mixed)
    cut_rows = count // 2
    d_near = [across(d_pair[1][:cut_rows])]
    b_keep, b_send = call(
        branch_parts, (8,),
        [
            whole, whole, pl.BlockSpec((1, heads, 256), lambda n: (n, 0, 0)),
            pl.BlockSpec((16, 2 * part, 256), lambda n: (0, 4 + n // 4, n % 4)),
        ],
        [columns(2 * count)] * 2, halves,
        (mixed, active, dense, everything),
        1,
    )
    column_sum = jnp.sum(cotangent.astype(WIDE) * valid, axis=0)
    column_sum = column_sum.reshape(4, 2, 4, 2, part)
    gv = (gv_part + gv_other).reshape(2, 4, 4, 2, 2, part).transpose(1, 3, 2, 4, 0, 5)
    gv = jnp.concatenate([gv.reshape(4, 2, 4, 2, 2 * part), column_sum], axis=4)
    gb = grad_qkv_bias.reshape(3, 2, 4, 2, -1).transpose(1, 2, 3, 0, 4).reshape(2, 1, 4, 2, n_bias)
    gb = lax.dynamic_update_slice(jnp.zeros((4, 2, 4, 2, n_bias), WIDE), gb, (2 * c, xh, 0, 0, 0))
    gu = grad_up_bias.reshape(4, 1, 4, 1, own_units)
    gu = lax.dynamic_update_slice(jnp.zeros((4, 2, 4, 2, own_units), WIDE), gu, (0, xh, 0, c, 0))
    n_v = 3 * part
    pack = jnp.concatenate([gv, gb, gu], axis=4).reshape(64, 1, n_v + n_bias + own_units)
    pack = jnp.pad(pack, ((0, 0), (0, 0), (0, 256 - pack.shape[2])))
    d_near[0], b_keep, b_send, pack = held(d_near[0], b_keep, b_send, pack)
    d_near.append(across(d_pair[1][cut_rows:]))
    b_pair = pair_sum(b_keep, swap(b_send, "c"))
    pack = lax.all_to_all(pack, ("y", "xh", "z", "c"), 0, 0, tiled=True)
    d_near[0], d_near[1], b_pair[0], b_pair[1], pack, g_dense, g_other = held(*d_near, *b_pair, pack, g_dense, g_other)
    pack = jnp.sum(pack, axis=0)
    g_dense = by_source(c, pick(g_dense, c, 4), g_other, 2)
    g_dense = g_dense.transpose(2, 3, 4, 0, 1, 5, 6).reshape(4, 2, 8 * part, 256)
    g_dense = jnp.roll(g_dense, -y, 0)
    hops = scatter_first(g_dense, "y")
    b_near = across(b_pair[1])
    d_own = wide_sum(d_pair[0], jnp.concatenate(d_near)).astype(LOW)
    d_last = swap(d_own, "mp")
    b_near, d_last, hops = held(b_near, d_last, hops)
    b_own = held(wide_sum(b_pair[0], b_near).astype(LOW))[0]
    b_last = [swap(b_own[:cut_rows], "mp")]
    last = scatter_last(g_dense, hops, "y")

    def half_rows(n):
        return pl.BlockSpec((count // 2, n), lambda i: (i, 0))

    input_grad = call(
        input_rows, (2,),
        [half_rows(model), half_rows(model), half_rows(1), half_rows(model), half_rows(model), full(4, model)],
        half_rows(model), struct((count, model), WIDE),
        (tokens, cotangent, valid, d_own, d_last, gains),
        1,
    )
    late, b_last[0], last, input_grad, b_own = held(late, b_last[0], last, input_grad, b_own)
    b_last.append(swap(b_own[cut_rows:], "mp"))

    back_cut = jnp.concatenate([late[: 4 * part, : 3 * heads], late[4 * part : 8 * part]], axis=1)
    back_cut = lax.all_to_all(back_cut.reshape(4, part, 3 * heads + units), ("xh", "c"), 0, 0, tiled=True)
    owned_dense = scatter_direct(scatter_join(g_dense, hops, last).reshape(4, 4 * part, 256), "z")
    output = (tokens.astype(WIDE) + wide_sum(b_own, jnp.concatenate(b_last)) + gains[2] + gains[3]).astype(LOW)
    output, back_cut, owned_dense = held(output, back_cut, owned_dense)
    vector_sum = pack[0, :n_v]
    owned_down = jnp.concatenate([late[8 * part : 10 * part], late[10 * part :]], axis=1).astype(WIDE)
    owned_dense = owned_dense.reshape(8, own_rows, 256).transpose(1, 0, 2).reshape(own_rows, model)
    got_vectors = vector_sum.reshape(3, part)
    owned_vectors = jnp.concatenate([got_vectors, got_vectors[2:]])
    owned_qkv_bias = pack[0, n_v : n_v + n_bias].reshape(qkv_bias.shape)
    owned_up_bias = pack[0, n_v + n_bias : n_v + n_bias + own_units]

    mine = (qkv_weight, qkv_first, qkv_second)
    new_qkv = call(
        update_qkv, (1,),
        [full(4, part, 3 * heads + units)] + [full(*x.shape) for x in mine],
        [full(*x.shape) for x in mine], [struct(x.shape, WIDE) for x in mine], (back_cut,) + mine,
    )
    mine = (up_weight, up_first, up_second)
    new_up = call(
        update_up, (1,),
        [full(4, part, 3 * heads + units)] + [full(*x.shape) for x in mine],
        [full(*x.shape) for x in mine], [struct(x.shape, WIDE) for x in mine], (back_cut,) + mine,
    )
    new_dense = adamw(dense_weight, dense_first, dense_second, owned_dense, 0.2, WEIGHT_DECAY)
    new_down = adamw(down_weight, down_first, down_second, owned_down, 0.03, WEIGHT_DECAY)
    new_qkv_bias = adamw(qkv_bias, qkv_bias_first, qkv_bias_second, owned_qkv_bias, 0.5, 0.0)
    new_up_bias = adamw(up_bias, up_bias_first, up_bias_second, owned_up_bias, 0.5, 0.0)
    new_vectors = adamw(vectors, vector_first, vector_second, owned_vectors, 0.5, 0.0)
    return (output, input_grad, *new_qkv, *new_dense, *new_up, *new_down, *new_qkv_bias, *new_up_bias, *new_vectors)


def solution(mesh):
    mesh = Mesh(mesh.devices.reshape(4, 2, 4, 2, 2), ("y", "xh", "z", "c", "mp"))
    dp = ("y", "xh", "z", "c")
    both = ("mp",) + dp
    weights = (P(None, dp, "mp"),) * 3 + (P(both, None),) * 3 + (P(dp, "mp"),) * 3 + (P(both, None),) * 3
    smalls = (P(None, both),) * 3 + (P(both),) * 3 + (P(None, dp),) * 3
    rows = P(dp, None)
    in_specs = (rows, rows, rows) + weights + smalls
    out_specs = (rows, rows) + weights + smalls
    return jax.shard_map(local, mesh=mesh, in_specs=in_specs, out_specs=out_specs, check_vma=False)
```

```python
import functools
import math

import jax
import jax.numpy as jnp
from jax import lax
from jax.experimental import pallas as pl
from jax.experimental.pallas import tpu as pltpu
from jax.sharding import Mesh, PartitionSpec as P

HEAD_DIM = 64
ROT_DIMS = 32
STEP = 10


BETA_ONE = 0.9
BETA_TWO = 0.95
ADAM_EPS = 1e-08
WEIGHT_DECAY = 0.1
NORM_EPS = 1e-05
MASKED = -1e30
GELU_COEF = 0.7978845608028654

LOW = jnp.bfloat16
WIDE = jnp.float32
RING = 4
MICROSECOND = 1100000000


def shift(x, axis, step):
    size = lax.axis_size(axis)
    return lax.ppermute(x, axis, [(i, (i + step) % size) for i in range(size)])


def swap(x, axis):
    return shift(x, axis, 1)


def across(x):
    return lax.ppermute(x, ("xh", "mp"), [(0, 3), (3, 0), (1, 2), (2, 1)])


def by_source(index, own, other, dim=0):
    low = jnp.where(index == 0, own, other)
    high = jnp.where(index == 0, other, own)
    return jnp.stack([low, high], axis=dim)


def pick(x, index, dim=0):
    return lax.dynamic_index_in_dim(x, index, dim, keepdims=False)


def wide_sum(*xs):
    return functools.reduce(lambda a, b: a + b, [x.astype(WIDE) for x in xs])


def scatter_direct(x, axis):
    me = lax.axis_index(axis)
    own, right, far, left = [pick(x, lax.rem(me + k, RING)) for k in range(RING)]
    return wide_sum(own, shift(right, axis, 1), shift(left, axis, -1), shift(far, axis, 2))


def scatter_first(x, axis):
    flat = x.reshape((2 * RING,) + x.shape[2:])
    return shift(flat[3:5], axis, 1), shift(flat[5:7], axis, -1)


def scatter_last(x, got, axis):
    from_left, from_right = got
    on_right = wide_sum(x[1, 0], from_left[1]).astype(LOW)
    on_left = wide_sum(x[3, 1], from_right[0]).astype(LOW)
    return shift(on_right, axis, 1), shift(on_left, axis, -1)


def scatter_join(x, got, last, kind=LOW):
    from_left, from_right = got
    top = wide_sum(x[0, 0], from_right[1], last[0])
    bottom = wide_sum(x[0, 1], from_left[0], last[1])
    return jnp.stack([top, bottom]).astype(kind)


def dot(a, b, da, db):
    return lax.dot_general(a, b, (((da,), (db,)), ((), ())), preferred_element_type=WIDE)


def call(kernel, grid, in_specs, out_specs, out_shape, args, flops=0, limit=48, scratch=(), aliases=None):
    moved = sum(a.size * a.dtype.itemsize for a in args) if flops > 1 else 1
    return pl.pallas_call(
        kernel,
        grid=grid,
        in_specs=in_specs,
        out_specs=out_specs,
        out_shape=out_shape,
        scratch_shapes=scratch,
        input_output_aliases=aliases or {},
        compiler_params=pltpu.CompilerParams(vmem_limit_bytes=limit * 1024 * 1024),
        cost_estimate=pl.CostEstimate(flops=flops, bytes_accessed=moved, transcendentals=0),
    )(*args)


def struct(shape, dtype):
    return jax.ShapeDtypeStruct(shape, dtype)


def full(*shape):
    return pl.BlockSpec(shape, lambda *i: (0,) * len(shape))


PLACES = [((y * 2 + xh) * 4 + z, (y * 4 + z) * 2 + xh) for y in range(4) for xh in range(2) for z in range(4)]
HERE = [here for here, _ in sorted(PLACES, key=lambda p: p[1])]
THERE = [there for _, there in sorted(PLACES)]


def reorder(x, order):
    return jnp.concatenate([x[:, 64 * k : 64 * (k + 1)] for k in order], axis=1)


def cut_columns(qkv_ref, up_ref, out_ref):
    for xh in range(2):
        for c in range(2):
            to = xh * 2 + c
            for w in range(3):
                for low in range(2):
                    at = (2 * c + low) * 256 + xh * 128
                    out_ref[to, :, w * 256 + low * 128 : w * 256 + (low + 1) * 128] = qkv_ref[w, :, at : at + 128].astype(LOW)
            for pair in range(8):
                y, z = pair // 2, 2 * (pair % 2)
                at = y * 1024 + xh * 512 + z * 128 + c * 64
                piece = jnp.concatenate([up_ref[:, at : at + 64], up_ref[:, at + 128 : at + 192]], axis=1)
                out_ref[to, :, 768 + pair * 128 : 768 + (pair + 1) * 128] = piece.astype(LOW)


def normalise(x):
    centered = x - jnp.mean(x, axis=-1, keepdims=True)
    inverse = lax.rsqrt(jnp.mean(centered * centered, axis=-1, keepdims=True) + NORM_EPS)
    return centered * inverse, inverse


def norm_rows(pair_ref, other_ref, gains_ref, normed_ref, scaled_ref, turned_ref):
    def run(ref):
        scaled, _ = normalise(ref[0].astype(WIDE))
        normed = reorder(scaled * gains_ref[0:1] + gains_ref[1:2], HERE)
        normed_ref[...] = normed.astype(LOW)
        scaled_ref[...] = reorder(scaled, HERE).astype(LOW)
        for k in range(8):
            turned_ref[k * 256 : (k + 1) * 256, :] = normed[:, k * 256 : (k + 1) * 256].T.astype(LOW)

    pl.when(pl.program_id(0) < 2)(lambda: run(pair_ref))
    pl.when(pl.program_id(0) >= 2)(lambda: run(other_ref))


def attention_grads(turned_ref, d_joined_ref, others, out_ref):
    width = d_joined_ref.shape[1]
    grad = dot(turned_ref[...], d_joined_ref[...], 1, 0).astype(LOW)
    blocks, size = out_ref.shape[:2]
    for k in range(blocks):
        out_ref[k, :, :width] = grad[k * size : (k + 1) * size]
        out_ref[k, :, width:] = jnp.zeros((size, out_ref.shape[2] - width), LOW)


def feed_forward(
    normed_ref, turned_ref, back_ref, up_ref, down_a_ref, down_b_ref, bias_ref,
    active_ref, d_hidden_ref, d_bias_ref, grads_out, up_ref_out, down_ref_out, sems,
):
    step, steps = pl.program_id(0), pl.num_programs(0)
    model = normed_ref.shape[1]
    half = model // 2
    width = active_ref.shape[1]
    slot = lax.rem(step, 2)

    def stores(slot, at):
        column = pl.multiple_of(at * width, width)
        return [
            pltpu.make_async_copy(
                up_ref_out.at[slot], grads_out.at[:, pl.ds(128, 128), pl.ds(column, width)], sems.at[slot, 0]
            ),
            pltpu.make_async_copy(
                down_ref_out.at[slot], grads_out.at[pl.ds(at * 4, 4), pl.ds(256, 128), :], sems.at[slot, 1]
            ),
        ]

    hidden = dot(normed_ref[...], up_ref[...].reshape(model, width), 1, 0) + bias_ref[...]
    down = jnp.concatenate([down_a_ref[...].reshape(width, half), down_b_ref[...].reshape(width, half)], axis=1)
    d_active = dot(back_ref[...], down, 1, 1)
    square = hidden * hidden
    inner = jnp.tanh(GELU_COEF * (hidden + 0.044715 * square * hidden))
    ends = 0.5 * (1.0 + inner)
    active = (hidden * ends).astype(LOW)
    slope = ends + 0.5 * hidden * (1.0 - inner * inner) * GELU_COEF * (1.0 + 3.0 * 0.044715 * square)
    d_hidden = (d_active * slope).astype(LOW)
    active_ref[...] = active
    d_hidden_ref[...] = d_hidden
    d_bias_ref[...] = jnp.sum(d_hidden.astype(WIDE), axis=0, keepdims=True)

    @pl.when(step >= 2)
    def _():
        for x in stores(slot, step - 2):
            x.wait()

    up_grad = dot(turned_ref[...], d_hidden, 1, 0).astype(LOW)
    down_grad = dot(active, back_ref[...], 0, 0).astype(LOW)
    for k in range(16):
        up_ref_out[slot, k] = up_grad[k * 128 : (k + 1) * 128]
    for z in range(4):
        down_ref_out[slot, z, :64] = down_grad[z * 64 : (z + 1) * 64, :half]
        down_ref_out[slot, z, 64:] = down_grad[z * 64 : (z + 1) * 64, half:]
    for x in stores(slot, step):
        x.start()

    @pl.when(step == steps - 1)
    def _():
        for x in stores(1 - slot, step - 1):
            x.wait()
        for x in stores(slot, step):
            x.wait()


def branch_parts(mixed_ref, active_ref, dense_ref, down_ref, keep_ref, send_ref):
    branch = dot(mixed_ref[...], dense_ref[0], 1, 0)
    branch += dot(active_ref[...], down_ref[...].reshape(active_ref.shape[1], -1), 1, 0)
    branch = branch.astype(LOW)
    half = branch.shape[0] // 2
    keep_ref[...] = branch[:half]
    send_ref[...] = branch[half:]


def normed_parts(d_joined_ref, d_hidden_ref, scaled_ref, qkv_ref, up_ref, keep_ref, send_ref, sums_ref):
    half, width = keep_ref.shape
    total = dot(d_joined_ref[...], qkv_ref[...].reshape(width, -1)[:, : d_joined_ref.shape[1]], 1, 1)
    total += dot(d_hidden_ref[...], up_ref[...].reshape(width, -1), 1, 1)
    low = total.astype(LOW)
    keep_ref[...] = low[:half]
    send_ref[...] = low[half:]
    sums_ref[0:1] = jnp.sum(total * scaled_ref[...].astype(WIDE), axis=0, keepdims=True)
    sums_ref[1:2] = jnp.sum(total, axis=0, keepdims=True)


def input_rows(tokens_ref, cotangent_ref, valid_ref, d_one_ref, d_two_ref, gains_ref, grad_ref):
    scaled, inverse = normalise(tokens_ref[...].astype(WIDE))
    upstream = cotangent_ref[...].astype(WIDE) * valid_ref[...]
    d_normed = reorder(d_one_ref[...].astype(WIDE) + d_two_ref[...].astype(WIDE), THERE)
    d_scaled = d_normed * gains_ref[0:1]
    grad_ref[...] = upstream + inverse * (
        d_scaled
        - jnp.mean(d_scaled, axis=-1, keepdims=True)
        - scaled * jnp.mean(d_scaled * scaled, axis=-1, keepdims=True)
    )


def update_qkv(grad_ref, weight_ref, first_ref, second_ref, *out_refs):
    for xh in range(2):
        for y in range(4):
            for w in range(3):
                at = slice(y * 256 + xh * 128, y * 256 + (xh + 1) * 128)
                here = w * 256 + (y % 2) * 128
                grad = grad_ref[xh * 2 + y // 2, :, here : here + 128].astype(WIDE)
                new = adamw(weight_ref[w, :, at], first_ref[w, :, at], second_ref[w, :, at], grad, 0.05, WEIGHT_DECAY)
                for ref, value in zip(out_refs, new):
                    ref[w, :, at] = value


def update_up(grad_ref, weight_ref, first_ref, second_ref, *out_refs):
    for xh in range(2):
        for y in range(4):
            for z in range(4):
                base = y * 1024 + xh * 512 + z * 128
                at = slice(base, base + 128)
                here = 768 + (y * 4 + z) * 64
                grad = jnp.concatenate(
                    [grad_ref[xh * 2 + c, :, here : here + 64].astype(WIDE) for c in range(2)], axis=1
                )
                new = adamw(weight_ref[:, at], first_ref[:, at], second_ref[:, at], grad, 0.05, WEIGHT_DECAY)
                for ref, value in zip(out_refs, new):
                    ref[:, at] = value


def held(*xs):
    return lax.optimization_barrier(xs)


def attend(
    normed_ref, weight_ref, bias_ref, back_ref, dense_ref, start_ref, cos_ref, sin_ref,
    mixed_ref, d_joined_ref, g_dense_ref, d_bias_ref, joined_ref, sum_ref,
):
    count, width = mixed_ref.shape
    weight = weight_ref[...].reshape(normed_ref.shape[1], -1)
    joined_ref[...] = lax.dot_general(normed_ref[...], weight, (((1,), (0,)), ((), ())), preferred_element_type=WIDE)
    back = back_ref[...]
    pieces = dense_ref.shape[0]
    dense = jnp.concatenate([dense_ref[k] for k in range(pieces)], axis=1)
    d_mixed = lax.dot_general(back, dense, (((1,), (1,)), ((), ())), preferred_element_type=WIDE).astype(LOW)
    heads = width // HEAD_DIM
    lanes = 128
    lane = lax.broadcasted_iota(jnp.int32, (count, lanes), 1) % HEAD_DIM
    cosine = cos_ref[...]
    sine = sin_ref[...]
    half = ROT_DIMS // 2
    low_sine = jnp.where(lane < half, sine, 0.0)
    high_sine = jnp.where((lane >= half) & (lane < ROT_DIMS), sine, 0.0)

    def turn(x, sign):
        up = pltpu.roll(x, half, 1) * high_sine
        down = pltpu.roll(x, lanes - half, 1) * low_sine
        return x * cosine + sign * (up - down)

    place = lax.broadcasted_iota(jnp.int32, (count, count), 0)
    other = lax.broadcasted_iota(jnp.int32, (count, count), 1)
    allowed = (other >= start_ref[...]) & (other <= place)
    scale = HEAD_DIM ** (-0.5)

    def dot(a, b, da, db):
        return lax.dot_general(a, b, (((da,), (db,)), ((), ())), preferred_element_type=WIDE)

    for pair in range(width // lanes):
        at = pair * lanes
        query2 = turn(joined_ref[:, at : at + lanes] + bias_ref[:, at : at + lanes], 1.0).astype(LOW)
        k_at = width + at
        keys2 = turn(joined_ref[:, k_at : k_at + lanes] + bias_ref[:, k_at : k_at + lanes], 1.0).astype(LOW)
        v_at = 2 * width + at
        values2 = (joined_ref[:, v_at : v_at + lanes] + bias_ref[:, v_at : v_at + lanes]).astype(LOW)
        d_out2 = d_mixed[:, at : at + lanes]
        mixed, d_query, d_keys, d_values = [], [], [], []
        for h in range(lanes // HEAD_DIM):
            cut = slice(h * HEAD_DIM, (h + 1) * HEAD_DIM)
            query, keys, values, d_out = query2[:, cut], keys2[:, cut], values2[:, cut], d_out2[:, cut]
            query = query * jnp.asarray(scale, LOW)
            scores = jnp.where(allowed, dot(query, keys, 1, 1), MASKED)
            expo = jnp.exp(scores - jnp.max(scores, axis=1, keepdims=True))
            weights = expo * (1.0 / jnp.sum(expo, axis=1, keepdims=True))
            weights_low = weights.astype(LOW)
            mixed.append(dot(weights_low, values, 1, 0))
            d_weights = dot(d_out, values, 1, 1)
            d_values.append(dot(weights_low, d_out, 0, 0))
            delta = jnp.sum(weights * d_weights, axis=1, keepdims=True)
            d_scores = (weights * (d_weights - delta)).astype(LOW)
            d_query.append(dot(d_scores, keys, 1, 0) * scale)
            d_keys.append(dot(d_scores, query, 0, 0))
        mixed_ref[:, at : at + lanes] = jnp.concatenate(mixed, axis=1).astype(LOW)
        d_joined_ref[:, at : at + lanes] = turn(jnp.concatenate(d_query, axis=1), -1.0).astype(LOW)
        d_joined_ref[:, k_at : k_at + lanes] = turn(jnp.concatenate(d_keys, axis=1), -1.0).astype(LOW)
        d_joined_ref[:, v_at : v_at + lanes] = jnp.concatenate(d_values, axis=1).astype(LOW)

    step = pl.program_id(0)

    @pl.when(step == 0)
    def _():
        sum_ref[...] = jnp.zeros_like(sum_ref)
        d_bias_ref[...] = jnp.zeros_like(d_bias_ref)

    sum_ref[...] += dot(mixed_ref[...], back, 0, 0)
    d_bias_ref[...] += jnp.sum(d_joined_ref[...].astype(WIDE), axis=0, keepdims=True)

    @pl.when(step == pl.num_programs(0) - 1)
    def _():
        size = back.shape[1] // pieces
        for k in range(pieces):
            g_dense_ref[k] = sum_ref[:, k * size : (k + 1) * size].astype(LOW)


def attention(normed, weights, bias, back, dense, start, cosine, sine, count):
    rows, model = back.shape
    width = dense.shape[1]

    def block(columns):
        return pl.BlockSpec((count, columns), lambda r: (r, 0))

    return pl.pallas_call(
        attend,
        grid=(rows // count,),
        in_specs=[
            block(model),
            pl.BlockSpec((16, model // 16, 3 * width), lambda r: (0, 0, 0)),
            pl.BlockSpec((1, 3 * width), lambda r: (0, 0)),
            block(model),
            pl.BlockSpec(dense.shape, lambda r: (0, 0, 0)),
            block(1),
            block(128),
            block(128),
        ],
        out_specs=[
            block(width),
            block(3 * width),
            pl.BlockSpec(dense.shape, lambda r: (0, 0, 0)),
            pl.BlockSpec((1, 3 * width), lambda r: (0, 0)),
        ],
        out_shape=[
            jax.ShapeDtypeStruct((rows, width), LOW),
            jax.ShapeDtypeStruct((rows, 3 * width), LOW),
            jax.ShapeDtypeStruct(dense.shape, LOW),
            jax.ShapeDtypeStruct((1, 3 * width), WIDE),
        ],
        scratch_shapes=[pltpu.VMEM((count, 3 * width), WIDE), pltpu.VMEM((width, model), WIDE)],
        compiler_params=pltpu.CompilerParams(vmem_limit_bytes=56 * 1024 * 1024),
        cost_estimate=pl.CostEstimate(flops=18 * MICROSECOND, bytes_accessed=rows * model * 2, transcendentals=0),
    )(normed, weights, bias, back, dense, start, cosine, sine)


def starts(lengths_row, count):
    finish = jnp.cumsum(lengths_row)
    place = jnp.arange(count, dtype=jnp.int32)
    passed = place[:, None] >= finish[None, :]
    start = jnp.max(jnp.where(passed, finish[None, :], 0), axis=1)
    return start, place < finish[-1]


def gelu(value):
    return 0.5 * value * (1.0 + jnp.tanh(GELU_COEF * (value + 0.044715 * value * value * value)))


def gelu_slope(value):
    inner = jnp.tanh(GELU_COEF * (value + 0.044715 * value * value * value))
    return 0.5 * (1.0 + inner) + 0.5 * value * (1.0 - inner * inner) * GELU_COEF * (
        1.0 + 3.0 * 0.044715 * value * value
    )


def adamw(weight, first, second, grad, rate, decay):
    first = BETA_ONE * first + (1.0 - BETA_ONE) * grad
    second = BETA_TWO * second + (1.0 - BETA_TWO) * grad * grad
    update = first / (1.0 - BETA_ONE**STEP) / (jnp.sqrt(second / (1.0 - BETA_TWO**STEP)) + ADAM_EPS)
    return (weight - rate * (update + decay * weight), first, second)


def local(
    tokens,
    cotangent,
    lengths,
    qkv_weight,
    qkv_first,
    qkv_second,
    dense_weight,
    dense_first,
    dense_second,
    up_weight,
    up_first,
    up_second,
    down_weight,
    down_first,
    down_second,
    qkv_bias,
    qkv_bias_first,
    qkv_bias_second,
    up_bias,
    up_bias_first,
    up_bias_second,
    vectors,
    vector_first,
    vector_second,
):
    xh, c = lax.axis_index("xh"), lax.axis_index("c")
    count, model = tokens.shape
    rows = 4 * count
    part = qkv_weight.shape[1]
    own_units = down_weight.shape[0]
    own_rows = dense_weight.shape[0]
    units = 16 * own_units
    heads = 256
    side = model // 2

    y, z = lax.axis_index("y"), lax.axis_index("z")
    cut = call(
        cut_columns, (1,),
        [full(*qkv_weight.shape), full(*up_weight.shape)],
        full(4, part, 3 * heads + units), struct((4, part, 3 * heads + units), LOW), (qkv_weight, up_weight),
    )
    cut = lax.all_to_all(cut, ("xh", "c"), 0, 0, tiled=True)
    dense_lines = dense_weight.astype(LOW).reshape(own_rows, 8, 256).transpose(1, 0, 2).reshape(2, 4 * own_rows, 256)
    down_low = down_weight.astype(LOW)
    q = cut[:, :, : 3 * heads]
    u = cut[:, :, 3 * heads :]
    payload = jnp.concatenate(
        [jnp.concatenate([q.reshape(4 * part, -1), dense_lines.reshape(4 * part, 256)], axis=1), u.reshape(4 * part, -1)]
        + [down_low[:, :side], down_low[:, side:]]
    )
    everything = lax.all_gather(payload, ("y", "z"), axis=0, tiled=False)

    n_vec = 4 * vectors.shape[1]
    n_bias = 3 * qkv_bias.shape[1]
    n_small = n_vec + n_bias + own_units
    small = [vectors.reshape(-1), qkv_bias.reshape(-1), up_bias, lengths[0].astype(WIDE)]
    small = jnp.concatenate(small).astype(LOW)
    small = jnp.pad(small, (0, 256 - small.shape[0]))
    small = jnp.broadcast_to(small[None, None], (64, 1, 256))
    payload, tokens_sent, small, cotangent, lengths = held(payload, tokens, small, cotangent, lengths)
    own_start, own_valid = starts(lengths[0], count)
    valid = own_valid[:, None].astype(WIDE)
    back_own = (cotangent.astype(WIDE) * valid).astype(LOW)

    small = lax.all_to_all(small, ("y", "xh", "z", "c"), 0, 0, tiled=True)

    tokens_near = across(tokens_sent)
    small, tokens_near = held(small, tokens_near)
    tokens_pair = jnp.stack([tokens, tokens_near])
    tokens_other = swap(tokens_pair, "c")
    tokens_other, back_own = held(tokens_other, back_own)
    back_near = across(back_own)
    back_pair = jnp.stack([back_own, back_near])
    back_other = swap(back_pair, "c")
    all_back = jnp.concatenate([back_pair, back_other]).reshape(rows, model)

    small = small.reshape(4, 2, 4, 2, 256).astype(WIDE)
    gains = small[..., :n_vec].reshape(64, 4, -1).transpose(1, 0, 2).reshape(4, model)
    in_chip = pick(small, xh, 1)
    b_qkv = in_chip[..., n_vec : n_vec + n_bias].reshape(2, 2, 4, 2, 3, -1)
    b_qkv = pick(b_qkv, c).transpose(3, 0, 1, 2, 4).reshape(1, 3 * heads)
    b_up = pick(in_chip, c, 2)[..., n_vec + n_bias : n_small].reshape(1, units)
    near = pick(pick(small, y), z, 1)[..., n_small : n_small + 4]
    order = [(xh, c), (1 - xh, c), (xh, 1 - c), (1 - xh, 1 - c)]
    all_lengths = jnp.stack([pick(pick(near, i), j) for i, j in order]).astype(jnp.int32)
    start, _ = jax.vmap(functools.partial(starts, count=count))(all_lengths)
    position = (jnp.arange(count, dtype=jnp.int32)[None, :] - start).reshape(-1, 1)
    start = start.reshape(-1, 1)
    half = ROT_DIMS // 2
    lane = jnp.arange(128, dtype=jnp.int32) % HEAD_DIM
    freq = 10000.0 ** (-2.0 * (lane % half).astype(WIDE) / (2 * half))
    angle = position.astype(WIDE) * freq[None, :]
    turned = (lane < ROT_DIMS)[None, :]
    cosine = jnp.where(turned, jnp.cos(angle), 1.0)
    sine = jnp.where(turned, jnp.sin(angle), 0.0)
    normed, scaled, turned_rows = call(
        norm_rows, (4,),
        [
            pl.BlockSpec((1, count, model), lambda i: (jnp.minimum(i, 1), 0, 0)),
            pl.BlockSpec((1, count, model), lambda i: (jnp.maximum(i - 2, 0), 0, 0)),
            full(4, model),
        ],
        [pl.BlockSpec((count, model), lambda i: (i, 0))] * 2 + [pl.BlockSpec((model, count), lambda i: (0, i))],
        [struct((rows, model), LOW)] * 2 + [struct((model, rows), LOW)],
        (tokens_pair, tokens_other, gains),
        8 * MICROSECOND,
    )
    everything, normed, scaled, turned_rows, cosine, sine, start, b_qkv, b_up, all_back = held(
        everything, normed, scaled, turned_rows, cosine, sine, start, b_qkv, b_up, all_back
    )

    def columns(n_rows):
        return pl.BlockSpec((n_rows, 256), lambda n: (0, n))

    whole = pl.BlockSpec(memory_space=pltpu.VMEM)
    anywhere = pl.BlockSpec(memory_space=pl.ANY)

    lines = everything[:, : 4 * part, 3 * heads :].reshape(2, 2, 4, 2, 4, own_rows, 256)
    other = swap(pick(lines, 1 - c), "c")
    active, d_hidden, grad_up_bias, grads = call(
        feed_forward, (4,),
        [
            whole, whole, whole,
            pl.BlockSpec((16, 4 * part, 256), lambda j: (0, 1, j)),
            pl.BlockSpec((4, 2 * part, side), lambda j: (j, 4, 0)),
            pl.BlockSpec((4, 2 * part, side), lambda j: (j, 5, 0)),
            columns(1),
        ],
        [columns(rows), columns(rows), columns(1), anywhere],
        [struct((rows, units), LOW)] * 2 + [struct((1, units), WIDE), struct((16, 12 * part, side), LOW)],
        (normed, turned_rows, all_back, everything, everything, everything, b_up),
        1, 56,
        [
            pltpu.VMEM((2, 16, 4 * part, 256), LOW),
            pltpu.VMEM((2, 4, 4 * part, side), LOW),
            pltpu.SemaphoreType.DMA((2, 2)),
        ],
    )
    active, d_hidden, grads, other, normed, all_back = held(active, d_hidden, grads, other, normed, all_back)
    lines = by_source(c, pick(lines, c), other, 2)
    dense = lines.transpose(3, 4, 0, 1, 2, 5, 6).reshape(8, heads, 256)
    mixed, d_joined, g_dense, grad_qkv_bias = attention(
        normed, everything, b_qkv, all_back, dense, start, cosine, sine, count
    )
    g_dense = g_dense.reshape(2, 4, 2, 4, 2, own_rows, 256)
    g_other = swap(pick(g_dense, 1 - c, 4), "c")
    grads = call(
        attention_grads, (4,),
        [pl.BlockSpec((512, rows), lambda n: (n, 0)), whole, anywhere],
        pl.BlockSpec((4, 4 * part, side), lambda n: (n, 0, 0)), struct((16, 12 * part, side), LOW),
        (turned_rows, d_joined, grads),
        1, 56, (), {2: 0},
    )
    grads, g_other, d_joined = held(grads, g_other, d_joined)

    late = lax.psum_scatter(grads.reshape(-1, side), ("y", "z"), scatter_dimension=0, tiled=True)

    def pair_sum(keep, got):
        return [wide_sum(keep[i * count : (i + 1) * count], got[i * count : (i + 1) * count]).astype(LOW) for i in range(2)]

    halves = [struct((2 * count, model), LOW)] * 2
    d_keep, d_send, gv_part = call(
        normed_parts, (8,),
        [
            whole, whole, columns(rows),
            pl.BlockSpec((2, 4 * part, side), lambda n: (n, 0, 0)),
            pl.BlockSpec((2, 4 * part, side), lambda n: (n, 1, 0)),
        ],
        [columns(2 * count)] * 2 + [columns(2)],
        halves + [struct((2, model), WIDE)],
        (d_joined, d_hidden, scaled, everything, everything),
        1,
    )
    d_keep, d_send, gv_part, mixed = held(d_keep, d_send, gv_part, mixed)

    d_pair = pair_sum(d_keep, swap(d_send, "c"))
    gv_other = swap(gv_part, "mp")
    d_pair[0], d_pair[1], gv_other, mixed = held(*d_pair, gv_other, mixed)
    cut_rows = count // 2
    d_near = [across(d_pair[1][:cut_rows])]
    b_keep, b_send = call(
        branch_parts, (8,),
        [
            whole, whole, pl.BlockSpec((1, heads, 256), lambda n: (n, 0, 0)),
            pl.BlockSpec((16, 2 * part, 256), lambda n: (0, 4 + n // 4, n % 4)),
        ],
        [columns(2 * count)] * 2, halves,
        (mixed, active, dense, everything),
        1,
    )
    column_sum = jnp.sum(cotangent.astype(WIDE) * valid, axis=0)
    column_sum = column_sum.reshape(4, 2, 4, 2, part)
    gv = (gv_part + gv_other).reshape(2, 4, 4, 2, 2, part).transpose(1, 3, 2, 4, 0, 5)
    gv = jnp.concatenate([gv.reshape(4, 2, 4, 2, 2 * part), column_sum], axis=4)
    gb = grad_qkv_bias.reshape(3, 2, 4, 2, -1).transpose(1, 2, 3, 0, 4).reshape(2, 1, 4, 2, n_bias)
    gb = lax.dynamic_update_slice(jnp.zeros((4, 2, 4, 2, n_bias), WIDE), gb, (2 * c, xh, 0, 0, 0))
    gu = grad_up_bias.reshape(4, 1, 4, 1, own_units)
    gu = lax.dynamic_update_slice(jnp.zeros((4, 2, 4, 2, own_units), WIDE), gu, (0, xh, 0, c, 0))
    n_v = 3 * part
    pack = jnp.concatenate([gv, gb, gu], axis=4).reshape(64, 1, n_v + n_bias + own_units)
    pack = jnp.pad(pack, ((0, 0), (0, 0), (0, 256 - pack.shape[2])))
    d_near[0], b_keep, b_send, pack = held(d_near[0], b_keep, b_send, pack)
    d_near.append(across(d_pair[1][cut_rows:]))
    b_pair = pair_sum(b_keep, swap(b_send, "c"))
    pack = lax.all_to_all(pack, ("y", "xh", "z", "c"), 0, 0, tiled=True)
    d_near[0], d_near[1], b_pair[0], b_pair[1], pack, g_dense, g_other = held(*d_near, *b_pair, pack, g_dense, g_other)
    pack = jnp.sum(pack, axis=0)
    g_dense = by_source(c, pick(g_dense, c, 4), g_other, 2)
    g_dense = g_dense.transpose(2, 3, 4, 0, 1, 5, 6).reshape(4, 2, 8 * part, 256)
    g_dense = jnp.roll(g_dense, -y, 0)
    hops = scatter_first(g_dense, "y")
    b_near = across(b_pair[1])
    d_own = wide_sum(d_pair[0], jnp.concatenate(d_near)).astype(LOW)
    d_last = swap(d_own, "mp")
    last = scatter_last(g_dense, hops, "y")
    b_near, d_last, last = held(b_near, d_last, last)
    b_own = held(wide_sum(b_pair[0], b_near).astype(LOW))[0]
    b_last = [swap(b_own[:cut_rows], "mp")]
    owned_dense = scatter_direct(scatter_join(g_dense, hops, last).reshape(4, 4 * part, 256), "z")

    def half_rows(n):
        return pl.BlockSpec((count // 2, n), lambda i: (i, 0))

    input_grad = call(
        input_rows, (2,),
        [half_rows(model), half_rows(model), half_rows(1), half_rows(model), half_rows(model), full(4, model)],
        half_rows(model), struct((count, model), WIDE),
        (tokens, cotangent, valid, d_own, d_last, gains),
        1,
    )
    late, b_last[0], owned_dense, input_grad, b_own = held(late, b_last[0], owned_dense, input_grad, b_own)

    back_cut = jnp.concatenate([late[: 4 * part, : 3 * heads], late[4 * part : 8 * part]], axis=1)
    back_cut, late, owned_dense, b_own, pack = held(back_cut, late, owned_dense, b_own, pack)
    back_cut = lax.all_to_all(back_cut.reshape(4, part, 3 * heads + units), ("xh", "c"), 0, 0, tiled=True)
    b_last.append(swap(b_own[cut_rows:], "mp"))
    output = (tokens.astype(WIDE) + wide_sum(b_own, jnp.concatenate(b_last)) + gains[2] + gains[3]).astype(LOW)
    output, back_cut = held(output, back_cut)
    vector_sum = pack[0, :n_v]
    owned_down = jnp.concatenate([late[8 * part : 10 * part], late[10 * part :]], axis=1).astype(WIDE)
    owned_dense = owned_dense.reshape(8, own_rows, 256).transpose(1, 0, 2).reshape(own_rows, model)
    got_vectors = vector_sum.reshape(3, part)
    owned_vectors = jnp.concatenate([got_vectors, got_vectors[2:]])
    owned_qkv_bias = pack[0, n_v : n_v + n_bias].reshape(qkv_bias.shape)
    owned_up_bias = pack[0, n_v + n_bias : n_v + n_bias + own_units]

    mine = (qkv_weight, qkv_first, qkv_second)
    new_qkv = call(
        update_qkv, (1,),
        [full(4, part, 3 * heads + units)] + [full(*x.shape) for x in mine],
        [full(*x.shape) for x in mine], [struct(x.shape, WIDE) for x in mine], (back_cut,) + mine,
    )
    mine = (up_weight, up_first, up_second)
    new_up = call(
        update_up, (1,),
        [full(4, part, 3 * heads + units)] + [full(*x.shape) for x in mine],
        [full(*x.shape) for x in mine], [struct(x.shape, WIDE) for x in mine], (back_cut,) + mine,
    )
    new_dense = adamw(dense_weight, dense_first, dense_second, owned_dense, 0.2, WEIGHT_DECAY)
    new_down = adamw(down_weight, down_first, down_second, owned_down, 0.03, WEIGHT_DECAY)
    new_qkv_bias = adamw(qkv_bias, qkv_bias_first, qkv_bias_second, owned_qkv_bias, 0.5, 0.0)
    new_up_bias = adamw(up_bias, up_bias_first, up_bias_second, owned_up_bias, 0.5, 0.0)
    new_vectors = adamw(vectors, vector_first, vector_second, owned_vectors, 0.5, 0.0)
    return (output, input_grad, *new_qkv, *new_dense, *new_up, *new_down, *new_qkv_bias, *new_up_bias, *new_vectors)


def solution(mesh):
    mesh = Mesh(mesh.devices.reshape(4, 2, 4, 2, 2), ("y", "xh", "z", "c", "mp"))
    dp = ("y", "xh", "z", "c")
    both = ("mp",) + dp
    weights = (P(None, dp, "mp"),) * 3 + (P(both, None),) * 3 + (P(dp, "mp"),) * 3 + (P(both, None),) * 3
    smalls = (P(None, both),) * 3 + (P(both),) * 3 + (P(None, dp),) * 3
    rows = P(dp, None)
    in_specs = (rows, rows, rows) + weights + smalls
    out_specs = (rows, rows) + weights + smalls
    return jax.shard_map(local, mesh=mesh, in_specs=in_specs, out_specs=out_specs, check_vma=False)
```

```python
import functools
import math

import jax
import jax.numpy as jnp
from jax import lax
from jax.experimental import pallas as pl
from jax.experimental.pallas import tpu as pltpu
from jax.sharding import Mesh, PartitionSpec as P

HEAD_DIM = 64
ROT_DIMS = 32
STEP = 10


BETA_ONE = 0.9
BETA_TWO = 0.95
ADAM_EPS = 1e-08
WEIGHT_DECAY = 0.1
NORM_EPS = 1e-05
MASKED = -1e30
GELU_COEF = 0.7978845608028654

LOW = jnp.bfloat16
WIDE = jnp.float32
RING = 4
MICROSECOND = 1100000000


def shift(x, axis, step):
    size = lax.axis_size(axis)
    return lax.ppermute(x, axis, [(i, (i + step) % size) for i in range(size)])


def swap(x, axis):
    return shift(x, axis, 1)


def across(x):
    return lax.ppermute(x, ("xh", "mp"), [(0, 3), (3, 0), (1, 2), (2, 1)])


def by_source(index, own, other, dim=0):
    low = jnp.where(index == 0, own, other)
    high = jnp.where(index == 0, other, own)
    return jnp.stack([low, high], axis=dim)


def pick(x, index, dim=0):
    return lax.dynamic_index_in_dim(x, index, dim, keepdims=False)


def wide_sum(*xs):
    return functools.reduce(lambda a, b: a + b, [x.astype(WIDE) for x in xs])


def scatter_direct(x, axis):
    me = lax.axis_index(axis)
    own, right, far, left = [pick(x, lax.rem(me + k, RING)) for k in range(RING)]
    return wide_sum(own, shift(right, axis, 1), shift(left, axis, -1), shift(far, axis, 2))


def scatter_first(x, axis):
    flat = x.reshape((2 * RING,) + x.shape[2:])
    return shift(flat[3:5], axis, 1), shift(flat[5:7], axis, -1)


def scatter_last(x, got, axis):
    from_left, from_right = got
    on_right = wide_sum(x[1, 0], from_left[1]).astype(LOW)
    on_left = wide_sum(x[3, 1], from_right[0]).astype(LOW)
    return shift(on_right, axis, 1), shift(on_left, axis, -1)


def scatter_join(x, got, last, kind=LOW):
    from_left, from_right = got
    top = wide_sum(x[0, 0], from_right[1], last[0])
    bottom = wide_sum(x[0, 1], from_left[0], last[1])
    return jnp.stack([top, bottom]).astype(kind)


def dot(a, b, da, db):
    return lax.dot_general(a, b, (((da,), (db,)), ((), ())), preferred_element_type=WIDE)


def call(kernel, grid, in_specs, out_specs, out_shape, args, flops=0, limit=48, scratch=(), aliases=None):
    moved = sum(a.size * a.dtype.itemsize for a in args) if flops > 1 else 1
    return pl.pallas_call(
        kernel,
        grid=grid,
        in_specs=in_specs,
        out_specs=out_specs,
        out_shape=out_shape,
        scratch_shapes=scratch,
        input_output_aliases=aliases or {},
        compiler_params=pltpu.CompilerParams(vmem_limit_bytes=limit * 1024 * 1024),
        cost_estimate=pl.CostEstimate(flops=flops, bytes_accessed=moved, transcendentals=0),
    )(*args)


def struct(shape, dtype):
    return jax.ShapeDtypeStruct(shape, dtype)


def full(*shape):
    return pl.BlockSpec(shape, lambda *i: (0,) * len(shape))


PLACES = [((y * 2 + xh) * 4 + z, (y * 4 + z) * 2 + xh) for y in range(4) for xh in range(2) for z in range(4)]
HERE = [here for here, _ in sorted(PLACES, key=lambda p: p[1])]
THERE = [there for _, there in sorted(PLACES)]


def reorder(x, order):
    return jnp.concatenate([x[:, 64 * k : 64 * (k + 1)] for k in order], axis=1)


def cut_columns(qkv_ref, up_ref, out_ref):
    for xh in range(2):
        for c in range(2):
            to = xh * 2 + c
            for w in range(3):
                for low in range(2):
                    at = (2 * c + low) * 256 + xh * 128
                    out_ref[to, :, w * 256 + low * 128 : w * 256 + (low + 1) * 128] = qkv_ref[w, :, at : at + 128].astype(LOW)
            for pair in range(8):
                y, z = pair // 2, 2 * (pair % 2)
                at = y * 1024 + xh * 512 + z * 128 + c * 64
                piece = jnp.concatenate([up_ref[:, at : at + 64], up_ref[:, at + 128 : at + 192]], axis=1)
                out_ref[to, :, 768 + pair * 128 : 768 + (pair + 1) * 128] = piece.astype(LOW)


def normalise(x):
    centered = x - jnp.mean(x, axis=-1, keepdims=True)
    inverse = lax.rsqrt(jnp.mean(centered * centered, axis=-1, keepdims=True) + NORM_EPS)
    return centered * inverse, inverse


def norm_rows(pair_ref, other_ref, gains_ref, normed_ref, scaled_ref, turned_ref):
    def run(ref):
        scaled, _ = normalise(ref[0].astype(WIDE))
        normed = reorder(scaled * gains_ref[0:1] + gains_ref[1:2], HERE)
        normed_ref[...] = normed.astype(LOW)
        scaled_ref[...] = reorder(scaled, HERE).astype(LOW)
        for k in range(8):
            turned_ref[k * 256 : (k + 1) * 256, :] = normed[:, k * 256 : (k + 1) * 256].T.astype(LOW)

    pl.when(pl.program_id(0) < 2)(lambda: run(pair_ref))
    pl.when(pl.program_id(0) >= 2)(lambda: run(other_ref))


def attention_grads(turned_ref, d_joined_ref, others, out_ref):
    width = d_joined_ref.shape[1]
    grad = dot(turned_ref[...], d_joined_ref[...], 1, 0).astype(LOW)
    blocks, size = out_ref.shape[:2]
    for k in range(blocks):
        out_ref[k, :, :width] = grad[k * size : (k + 1) * size]
        out_ref[k, :, width:] = jnp.zeros((size, out_ref.shape[2] - width), LOW)


def feed_forward(
    normed_ref, turned_ref, back_ref, up_ref, down_a_ref, down_b_ref, bias_ref,
    active_ref, d_hidden_ref, d_bias_ref, grads_out, up_ref_out, down_ref_out, sems,
):
    step, steps = pl.program_id(0), pl.num_programs(0)
    model = normed_ref.shape[1]
    half = model // 2
    width = active_ref.shape[1]
    slot = lax.rem(step, 2)

    def stores(slot, at):
        column = pl.multiple_of(at * width, width)
        return [
            pltpu.make_async_copy(
                up_ref_out.at[slot], grads_out.at[:, pl.ds(128, 128), pl.ds(column, width)], sems.at[slot, 0]
            ),
            pltpu.make_async_copy(
                down_ref_out.at[slot], grads_out.at[pl.ds(at * 4, 4), pl.ds(256, 128), :], sems.at[slot, 1]
            ),
        ]

    hidden = dot(normed_ref[...], up_ref[...].reshape(model, width), 1, 0) + bias_ref[...]
    down = jnp.concatenate([down_a_ref[...].reshape(width, half), down_b_ref[...].reshape(width, half)], axis=1)
    d_active = dot(back_ref[...], down, 1, 1)
    square = hidden * hidden
    inner = jnp.tanh(GELU_COEF * (hidden + 0.044715 * square * hidden))
    ends = 0.5 * (1.0 + inner)
    active = (hidden * ends).astype(LOW)
    slope = ends + 0.5 * hidden * (1.0 - inner * inner) * GELU_COEF * (1.0 + 3.0 * 0.044715 * square)
    d_hidden = (d_active * slope).astype(LOW)
    active_ref[...] = active
    d_hidden_ref[...] = d_hidden
    d_bias_ref[...] = jnp.sum(d_hidden.astype(WIDE), axis=0, keepdims=True)

    @pl.when(step >= 2)
    def _():
        for x in stores(slot, step - 2):
            x.wait()

    up_grad = dot(turned_ref[...], d_hidden, 1, 0).astype(LOW)
    down_grad = dot(active, back_ref[...], 0, 0).astype(LOW)
    for k in range(16):
        up_ref_out[slot, k] = up_grad[k * 128 : (k + 1) * 128]
    for z in range(4):
        down_ref_out[slot, z, :64] = down_grad[z * 64 : (z + 1) * 64, :half]
        down_ref_out[slot, z, 64:] = down_grad[z * 64 : (z + 1) * 64, half:]
    for x in stores(slot, step):
        x.start()

    @pl.when(step == steps - 1)
    def _():
        for x in stores(1 - slot, step - 1):
            x.wait()
        for x in stores(slot, step):
            x.wait()


def branch_parts(mixed_ref, active_ref, dense_ref, down_ref, keep_ref, send_ref):
    branch = dot(mixed_ref[...], dense_ref[0], 1, 0)
    branch += dot(active_ref[...], down_ref[...].reshape(active_ref.shape[1], -1), 1, 0)
    branch = branch.astype(LOW)
    half = branch.shape[0] // 2
    keep_ref[...] = branch[:half]
    send_ref[...] = branch[half:]


def normed_parts(d_joined_ref, d_hidden_ref, scaled_ref, qkv_ref, up_ref, keep_ref, send_ref, sums_ref):
    half, width = keep_ref.shape
    total = dot(d_joined_ref[...], qkv_ref[...].reshape(width, -1)[:, : d_joined_ref.shape[1]], 1, 1)
    total += dot(d_hidden_ref[...], up_ref[...].reshape(width, -1), 1, 1)
    low = total.astype(LOW)
    keep_ref[...] = low[:half]
    send_ref[...] = low[half:]
    sums_ref[0:1] = jnp.sum(total * scaled_ref[...].astype(WIDE), axis=0, keepdims=True)
    sums_ref[1:2] = jnp.sum(total, axis=0, keepdims=True)


def input_rows(tokens_ref, cotangent_ref, valid_ref, d_one_ref, d_two_ref, gains_ref, grad_ref):
    scaled, inverse = normalise(tokens_ref[...].astype(WIDE))
    upstream = cotangent_ref[...].astype(WIDE) * valid_ref[...]
    d_normed = reorder(d_one_ref[...].astype(WIDE) + d_two_ref[...].astype(WIDE), THERE)
    d_scaled = d_normed * gains_ref[0:1]
    grad_ref[...] = upstream + inverse * (
        d_scaled
        - jnp.mean(d_scaled, axis=-1, keepdims=True)
        - scaled * jnp.mean(d_scaled * scaled, axis=-1, keepdims=True)
    )


def update_qkv(grad_ref, weight_ref, first_ref, second_ref, *out_refs):
    for xh in range(2):
        for y in range(4):
            for w in range(3):
                at = slice(y * 256 + xh * 128, y * 256 + (xh + 1) * 128)
                here = w * 256 + (y % 2) * 128
                grad = grad_ref[xh * 2 + y // 2, :, here : here + 128].astype(WIDE)
                new = adamw(weight_ref[w, :, at], first_ref[w, :, at], second_ref[w, :, at], grad, 0.05, WEIGHT_DECAY)
                for ref, value in zip(out_refs, new):
                    ref[w, :, at] = value


def update_up(grad_ref, weight_ref, first_ref, second_ref, *out_refs):
    for xh in range(2):
        for y in range(4):
            for z in range(4):
                base = y * 1024 + xh * 512 + z * 128
                at = slice(base, base + 128)
                here = 768 + (y * 4 + z) * 64
                grad = jnp.concatenate(
                    [grad_ref[xh * 2 + c, :, here : here + 64].astype(WIDE) for c in range(2)], axis=1
                )
                new = adamw(weight_ref[:, at], first_ref[:, at], second_ref[:, at], grad, 0.05, WEIGHT_DECAY)
                for ref, value in zip(out_refs, new):
                    ref[:, at] = value


def held(*xs):
    return lax.optimization_barrier(xs)


def attend(
    normed_ref, weight_ref, bias_ref, back_ref, dense_ref, start_ref, cos_ref, sin_ref,
    mixed_ref, d_joined_ref, g_dense_ref, d_bias_ref, joined_ref, sum_ref,
):
    count, width = mixed_ref.shape
    weight = weight_ref[...].reshape(normed_ref.shape[1], -1)
    joined_ref[...] = lax.dot_general(normed_ref[...], weight, (((1,), (0,)), ((), ())), preferred_element_type=WIDE)
    back = back_ref[...]
    pieces = dense_ref.shape[0]
    dense = jnp.concatenate([dense_ref[k] for k in range(pieces)], axis=1)
    d_mixed = lax.dot_general(back, dense, (((1,), (1,)), ((), ())), preferred_element_type=WIDE).astype(LOW)
    heads = width // HEAD_DIM
    lanes = 128
    lane = lax.broadcasted_iota(jnp.int32, (count, lanes), 1) % HEAD_DIM
    cosine = cos_ref[...]
    sine = sin_ref[...]
    half = ROT_DIMS // 2
    low_sine = jnp.where(lane < half, sine, 0.0)
    high_sine = jnp.where((lane >= half) & (lane < ROT_DIMS), sine, 0.0)

    def turn(x, sign):
        up = pltpu.roll(x, half, 1) * high_sine
        down = pltpu.roll(x, lanes - half, 1) * low_sine
        return x * cosine + sign * (up - down)

    place = lax.broadcasted_iota(jnp.int32, (count, count), 0)
    other = lax.broadcasted_iota(jnp.int32, (count, count), 1)
    allowed = (other >= start_ref[:, :1]) & (other <= place)
    scale = HEAD_DIM ** (-0.5)

    def dot(a, b, da, db):
        return lax.dot_general(a, b, (((da,), (db,)), ((), ())), preferred_element_type=WIDE)

    for pair in range(width // lanes):
        at = pair * lanes
        query2 = turn(joined_ref[:, at : at + lanes] + bias_ref[:, at : at + lanes], 1.0).astype(LOW)
        k_at = width + at
        keys2 = turn(joined_ref[:, k_at : k_at + lanes] + bias_ref[:, k_at : k_at + lanes], 1.0).astype(LOW)
        v_at = 2 * width + at
        values2 = (joined_ref[:, v_at : v_at + lanes] + bias_ref[:, v_at : v_at + lanes]).astype(LOW)
        d_out2 = d_mixed[:, at : at + lanes]
        mixed, d_query, d_keys, d_values = [], [], [], []
        for h in range(lanes // HEAD_DIM):
            cut = slice(h * HEAD_DIM, (h + 1) * HEAD_DIM)
            query, keys, values, d_out = query2[:, cut], keys2[:, cut], values2[:, cut], d_out2[:, cut]
            query = query * jnp.asarray(scale, LOW)
            scores = jnp.where(allowed, dot(query, keys, 1, 1), MASKED)
            expo = jnp.exp(scores - jnp.max(scores, axis=1, keepdims=True))
            weights = expo * (1.0 / jnp.sum(expo, axis=1, keepdims=True))
            weights_low = weights.astype(LOW)
            mixed.append(dot(weights_low, values, 1, 0))
            d_weights = dot(d_out, values, 1, 1)
            d_values.append(dot(weights_low, d_out, 0, 0))
            delta = jnp.sum(weights * d_weights, axis=1, keepdims=True)
            d_scores = (weights * (d_weights - delta)).astype(LOW)
            d_query.append(dot(d_scores, keys, 1, 0) * scale)
            d_keys.append(dot(d_scores, query, 0, 0))
        mixed_ref[:, at : at + lanes] = jnp.concatenate(mixed, axis=1).astype(LOW)
        d_joined_ref[:, at : at + lanes] = turn(jnp.concatenate(d_query, axis=1), -1.0).astype(LOW)
        d_joined_ref[:, k_at : k_at + lanes] = turn(jnp.concatenate(d_keys, axis=1), -1.0).astype(LOW)
        d_joined_ref[:, v_at : v_at + lanes] = jnp.concatenate(d_values, axis=1).astype(LOW)

    step = pl.program_id(0)

    @pl.when(step == 0)
    def _():
        sum_ref[...] = jnp.zeros_like(sum_ref)
        d_bias_ref[...] = jnp.zeros_like(d_bias_ref)

    sum_ref[...] += dot(mixed_ref[...], back, 0, 0)
    d_bias_ref[...] += jnp.sum(d_joined_ref[...].astype(WIDE), axis=0, keepdims=True)

    @pl.when(step == pl.num_programs(0) - 1)
    def _():
        size = back.shape[1] // pieces
        for k in range(pieces):
            g_dense_ref[k] = sum_ref[:, k * size : (k + 1) * size].astype(LOW)


def attention(normed, weights, bias, back, dense, start, cosine, sine, count):
    rows, model = back.shape
    width = dense.shape[1]

    def block(columns):
        return pl.BlockSpec((count, columns), lambda r: (r, 0))

    return pl.pallas_call(
        attend,
        grid=(rows // count,),
        in_specs=[
            block(model),
            pl.BlockSpec((16, model // 16, 3 * width), lambda r: (0, 0, 0)),
            pl.BlockSpec((1, 3 * width), lambda r: (0, 0)),
            block(model),
            pl.BlockSpec(dense.shape, lambda r: (0, 0, 0)),
            block(128),
            block(128),
            block(128),
        ],
        out_specs=[
            block(width),
            block(3 * width),
            pl.BlockSpec(dense.shape, lambda r: (0, 0, 0)),
            pl.BlockSpec((1, 3 * width), lambda r: (0, 0)),
        ],
        out_shape=[
            jax.ShapeDtypeStruct((rows, width), LOW),
            jax.ShapeDtypeStruct((rows, 3 * width), LOW),
            jax.ShapeDtypeStruct(dense.shape, LOW),
            jax.ShapeDtypeStruct((1, 3 * width), WIDE),
        ],
        scratch_shapes=[pltpu.VMEM((count, 3 * width), WIDE), pltpu.VMEM((width, model), WIDE)],
        compiler_params=pltpu.CompilerParams(vmem_limit_bytes=56 * 1024 * 1024),
        cost_estimate=pl.CostEstimate(flops=18 * MICROSECOND, bytes_accessed=rows * model * 2, transcendentals=0),
    )(normed, weights, bias, back, dense, start, cosine, sine)


def starts(lengths_row, count):
    finish = jnp.cumsum(lengths_row)
    place = jnp.arange(count, dtype=jnp.int32)
    passed = place[:, None] >= finish[None, :]
    start = jnp.max(jnp.where(passed, finish[None, :], 0), axis=1)
    return start, place < finish[-1]


def gelu(value):
    return 0.5 * value * (1.0 + jnp.tanh(GELU_COEF * (value + 0.044715 * value * value * value)))


def gelu_slope(value):
    inner = jnp.tanh(GELU_COEF * (value + 0.044715 * value * value * value))
    return 0.5 * (1.0 + inner) + 0.5 * value * (1.0 - inner * inner) * GELU_COEF * (
        1.0 + 3.0 * 0.044715 * value * value
    )


def adamw(weight, first, second, grad, rate, decay):
    first = BETA_ONE * first + (1.0 - BETA_ONE) * grad
    second = BETA_TWO * second + (1.0 - BETA_TWO) * grad * grad
    update = first / (1.0 - BETA_ONE**STEP) / (jnp.sqrt(second / (1.0 - BETA_TWO**STEP)) + ADAM_EPS)
    return (weight - rate * (update + decay * weight), first, second)


def local(
    tokens,
    cotangent,
    lengths,
    qkv_weight,
    qkv_first,
    qkv_second,
    dense_weight,
    dense_first,
    dense_second,
    up_weight,
    up_first,
    up_second,
    down_weight,
    down_first,
    down_second,
    qkv_bias,
    qkv_bias_first,
    qkv_bias_second,
    up_bias,
    up_bias_first,
    up_bias_second,
    vectors,
    vector_first,
    vector_second,
):
    xh, c = lax.axis_index("xh"), lax.axis_index("c")
    count, model = tokens.shape
    rows = 4 * count
    part = qkv_weight.shape[1]
    own_units = down_weight.shape[0]
    own_rows = dense_weight.shape[0]
    units = 16 * own_units
    heads = 256
    side = model // 2

    y, z = lax.axis_index("y"), lax.axis_index("z")
    cut = call(
        cut_columns, (1,),
        [full(*qkv_weight.shape), full(*up_weight.shape)],
        full(4, part, 3 * heads + units), struct((4, part, 3 * heads + units), LOW), (qkv_weight, up_weight),
    )
    cut = lax.all_to_all(cut, ("xh", "c"), 0, 0, tiled=True)
    dense_lines = dense_weight.astype(LOW).reshape(own_rows, 8, 256).transpose(1, 0, 2).reshape(2, 4 * own_rows, 256)
    down_low = down_weight.astype(LOW)
    q = cut[:, :, : 3 * heads]
    u = cut[:, :, 3 * heads :]
    payload = jnp.concatenate(
        [jnp.concatenate([q.reshape(4 * part, -1), dense_lines.reshape(4 * part, 256)], axis=1), u.reshape(4 * part, -1)]
        + [down_low[:, :side], down_low[:, side:]]
    )
    everything = lax.all_gather(payload, ("y", "z"), axis=0, tiled=False)

    n_vec = 4 * vectors.shape[1]
    n_bias = 3 * qkv_bias.shape[1]
    n_small = n_vec + n_bias + own_units
    small = [vectors.reshape(-1), qkv_bias.reshape(-1), up_bias, lengths[0].astype(WIDE)]
    small = jnp.concatenate(small).astype(LOW)
    small = jnp.pad(small, (0, 256 - small.shape[0]))
    small = jnp.broadcast_to(small[None, None], (64, 1, 256))
    payload, tokens_sent, small, cotangent, lengths = held(payload, tokens, small, cotangent, lengths)
    own_start, own_valid = starts(lengths[0], count)
    valid = own_valid[:, None].astype(WIDE)
    back_own = (cotangent.astype(WIDE) * valid).astype(LOW)

    small = lax.all_to_all(small, ("y", "xh", "z", "c"), 0, 0, tiled=True)

    tokens_near = across(tokens_sent)
    small, tokens_near = held(small, tokens_near)
    tokens_pair = jnp.stack([tokens, tokens_near])
    tokens_other = swap(tokens_pair, "c")
    tokens_other, back_own = held(tokens_other, back_own)
    back_near = across(back_own)
    back_pair = jnp.stack([back_own, back_near])
    back_other = swap(back_pair, "c")
    all_back = jnp.concatenate([back_pair, back_other]).reshape(rows, model)

    small = small.reshape(4, 2, 4, 2, 256).astype(WIDE)
    gains = small[..., :n_vec].reshape(64, 4, -1).transpose(1, 0, 2).reshape(4, model)
    in_chip = pick(small, xh, 1)
    b_qkv = in_chip[..., n_vec : n_vec + n_bias].reshape(2, 2, 4, 2, 3, -1)
    b_qkv = pick(b_qkv, c).transpose(3, 0, 1, 2, 4).reshape(1, 3 * heads)
    b_up = pick(in_chip, c, 2)[..., n_vec + n_bias : n_small].reshape(1, units)
    near = pick(pick(small, y), z, 1)[..., n_small : n_small + 4]
    order = [(xh, c), (1 - xh, c), (xh, 1 - c), (1 - xh, 1 - c)]
    all_lengths = jnp.stack([pick(pick(near, i), j) for i, j in order]).astype(jnp.int32)
    start, _ = jax.vmap(functools.partial(starts, count=count))(all_lengths)
    position = (jnp.arange(count, dtype=jnp.int32)[None, :] - start).reshape(-1, 1)
    start = jnp.broadcast_to(start.reshape(-1, 1), (rows, 128))
    half = ROT_DIMS // 2
    lane = jnp.arange(128, dtype=jnp.int32) % HEAD_DIM
    freq = 10000.0 ** (-2.0 * (lane % half).astype(WIDE) / (2 * half))
    angle = position.astype(WIDE) * freq[None, :]
    turned = (lane < ROT_DIMS)[None, :]
    cosine = jnp.where(turned, jnp.cos(angle), 1.0)
    sine = jnp.where(turned, jnp.sin(angle), 0.0)
    normed, scaled, turned_rows = call(
        norm_rows, (4,),
        [
            pl.BlockSpec((1, count, model), lambda i: (jnp.minimum(i, 1), 0, 0)),
            pl.BlockSpec((1, count, model), lambda i: (jnp.maximum(i - 2, 0), 0, 0)),
            full(4, model),
        ],
        [pl.BlockSpec((count, model), lambda i: (i, 0))] * 2 + [pl.BlockSpec((model, count), lambda i: (0, i))],
        [struct((rows, model), LOW)] * 2 + [struct((model, rows), LOW)],
        (tokens_pair, tokens_other, gains),
        8 * MICROSECOND,
    )
    everything, normed, scaled, turned_rows, cosine, sine, start, b_qkv, b_up, all_back = held(
        everything, normed, scaled, turned_rows, cosine, sine, start, b_qkv, b_up, all_back
    )

    def columns(n_rows):
        return pl.BlockSpec((n_rows, 256), lambda n: (0, n))

    whole = pl.BlockSpec(memory_space=pltpu.VMEM)
    anywhere = pl.BlockSpec(memory_space=pl.ANY)

    lines = everything[:, : 4 * part, 3 * heads :].reshape(2, 2, 4, 2, 4, own_rows, 256)
    other = swap(pick(lines, 1 - c), "c")
    active, d_hidden, grad_up_bias, grads = call(
        feed_forward, (4,),
        [
            whole, whole, whole,
            pl.BlockSpec((16, 4 * part, 256), lambda j: (0, 1, j)),
            pl.BlockSpec((4, 2 * part, side), lambda j: (j, 4, 0)),
            pl.BlockSpec((4, 2 * part, side), lambda j: (j, 5, 0)),
            columns(1),
        ],
        [columns(rows), columns(rows), columns(1), anywhere],
        [struct((rows, units), LOW)] * 2 + [struct((1, units), WIDE), struct((16, 12 * part, side), LOW)],
        (normed, turned_rows, all_back, everything, everything, everything, b_up),
        1, 56,
        [
            pltpu.VMEM((2, 16, 4 * part, 256), LOW),
            pltpu.VMEM((2, 4, 4 * part, side), LOW),
            pltpu.SemaphoreType.DMA((2, 2)),
        ],
    )
    active, d_hidden, grads, other, normed, all_back = held(active, d_hidden, grads, other, normed, all_back)
    lines = by_source(c, pick(lines, c), other, 2)
    dense = lines.transpose(3, 4, 0, 1, 2, 5, 6).reshape(8, heads, 256)
    mixed, d_joined, g_dense, grad_qkv_bias = attention(
        normed, everything, b_qkv, all_back, dense, start, cosine, sine, count
    )
    g_dense = g_dense.reshape(2, 4, 2, 4, 2, own_rows, 256)
    grads = call(
        attention_grads, (4,),
        [pl.BlockSpec((512, rows), lambda n: (n, 0)), whole, anywhere],
        pl.BlockSpec((4, 4 * part, side), lambda n: (n, 0, 0)), struct((16, 12 * part, side), LOW),
        (turned_rows, d_joined, grads),
        1, 56, (), {2: 0},
    )
    grads, g_dense, d_joined = held(grads, g_dense, d_joined)

    late = lax.psum_scatter(grads.reshape(-1, side), ("y", "z"), scatter_dimension=0, tiled=True)

    def pair_sum(keep, got):
        return [wide_sum(keep[i * count : (i + 1) * count], got[i * count : (i + 1) * count]).astype(LOW) for i in range(2)]

    halves = [struct((2 * count, model), LOW)] * 2
    d_keep, d_send, gv_part = call(
        normed_parts, (8,),
        [
            whole, whole, columns(rows),
            pl.BlockSpec((2, 4 * part, side), lambda n: (n, 0, 0)),
            pl.BlockSpec((2, 4 * part, side), lambda n: (n, 1, 0)),
        ],
        [columns(2 * count)] * 2 + [columns(2)],
        halves + [struct((2, model), WIDE)],
        (d_joined, d_hidden, scaled, everything, everything),
        1,
    )
    d_keep, d_send, gv_part, mixed = held(d_keep, d_send, gv_part, mixed)

    d_pair = pair_sum(d_keep, swap(d_send, "c"))
    gv_other = swap(gv_part, "mp")
    d_pair[0], d_pair[1], gv_other, mixed = held(*d_pair, gv_other, mixed)
    cut_rows = count // 2
    d_near = [across(d_pair[1][:cut_rows])]
    b_keep, b_send = call(
        branch_parts, (8,),
        [
            whole, whole, pl.BlockSpec((1, heads, 256), lambda n: (n, 0, 0)),
            pl.BlockSpec((16, 2 * part, 256), lambda n: (0, 4 + n // 4, n % 4)),
        ],
        [columns(2 * count)] * 2, halves,
        (mixed, active, dense, everything),
        1,
    )
    column_sum = jnp.sum(cotangent.astype(WIDE) * valid, axis=0)
    column_sum = column_sum.reshape(4, 2, 4, 2, part)
    gv = (gv_part + gv_other).reshape(2, 4, 4, 2, 2, part).transpose(1, 3, 2, 4, 0, 5)
    gv = jnp.concatenate([gv.reshape(4, 2, 4, 2, 2 * part), column_sum], axis=4)
    gb = grad_qkv_bias.reshape(3, 2, 4, 2, -1).transpose(1, 2, 3, 0, 4).reshape(2, 1, 4, 2, n_bias)
    gb = lax.dynamic_update_slice(jnp.zeros((4, 2, 4, 2, n_bias), WIDE), gb, (2 * c, xh, 0, 0, 0))
    gu = grad_up_bias.reshape(4, 1, 4, 1, own_units)
    gu = lax.dynamic_update_slice(jnp.zeros((4, 2, 4, 2, own_units), WIDE), gu, (0, xh, 0, c, 0))
    n_v = 3 * part
    pack = jnp.concatenate([gv, gb, gu], axis=4).reshape(64, 1, n_v + n_bias + own_units)
    pack = jnp.pad(pack, ((0, 0), (0, 0), (0, 256 - pack.shape[2])))
    d_near[0], b_keep, b_send, pack, g_dense = held(d_near[0], b_keep, b_send, pack, g_dense)
    d_near.append(across(d_pair[1][cut_rows:]))
    b_pair = pair_sum(b_keep, swap(b_send, "c"))
    pack = lax.all_to_all(pack, ("y", "xh", "z", "c"), 0, 0, tiled=True)
    g_other = swap(pick(g_dense, 1 - c, 4), "c")
    d_near[0], d_near[1], b_pair[0], b_pair[1], pack, g_dense, g_other = held(*d_near, *b_pair, pack, g_dense, g_other)
    pack = jnp.sum(pack, axis=0)
    g_dense = by_source(c, pick(g_dense, c, 4), g_other, 2)
    g_dense = g_dense.transpose(2, 3, 4, 0, 1, 5, 6).reshape(4, 2, 8 * part, 256)
    g_dense = jnp.roll(g_dense, -y, 0)
    hops = scatter_first(g_dense, "y")
    b_near = across(b_pair[1])
    d_own = wide_sum(d_pair[0], jnp.concatenate(d_near)).astype(LOW)
    d_last = swap(d_own, "mp")
    last = scatter_last(g_dense, hops, "y")
    b_near, d_last, last = held(b_near, d_last, last)
    b_own = held(wide_sum(b_pair[0], b_near).astype(LOW))[0]
    b_last = [swap(b_own[:cut_rows], "mp")]
    owned_dense = scatter_direct(scatter_join(g_dense, hops, last).reshape(4, 4 * part, 256), "z")

    def half_rows(n):
        return pl.BlockSpec((count // 2, n), lambda i: (i, 0))

    input_grad = call(
        input_rows, (2,),
        [half_rows(model), half_rows(model), half_rows(1), half_rows(model), half_rows(model), full(4, model)],
        half_rows(model), struct((count, model), WIDE),
        (tokens, cotangent, valid, d_own, d_last, gains),
        1,
    )
    late, b_last[0], owned_dense, input_grad, b_own = held(late, b_last[0], owned_dense, input_grad, b_own)

    back_cut = jnp.concatenate([late[: 4 * part, : 3 * heads], late[4 * part : 8 * part]], axis=1)
    back_cut, late, owned_dense, b_own, pack = held(back_cut, late, owned_dense, b_own, pack)
    back_cut = lax.all_to_all(back_cut.reshape(4, part, 3 * heads + units), ("xh", "c"), 0, 0, tiled=True)
    b_last.append(swap(b_own[cut_rows:], "mp"))
    output = (tokens.astype(WIDE) + wide_sum(b_own, jnp.concatenate(b_last)) + gains[2] + gains[3]).astype(LOW)
    output, back_cut = held(output, back_cut)
    vector_sum = pack[0, :n_v]
    owned_down = jnp.concatenate([late[8 * part : 10 * part], late[10 * part :]], axis=1).astype(WIDE)
    owned_dense = owned_dense.reshape(8, own_rows, 256).transpose(1, 0, 2).reshape(own_rows, model)
    got_vectors = vector_sum.reshape(3, part)
    owned_vectors = jnp.concatenate([got_vectors, got_vectors[2:]])
    owned_qkv_bias = pack[0, n_v : n_v + n_bias].reshape(qkv_bias.shape)
    owned_up_bias = pack[0, n_v + n_bias : n_v + n_bias + own_units]

    mine = (qkv_weight, qkv_first, qkv_second)
    new_qkv = call(
        update_qkv, (1,),
        [full(4, part, 3 * heads + units)] + [full(*x.shape) for x in mine],
        [full(*x.shape) for x in mine], [struct(x.shape, WIDE) for x in mine], (back_cut,) + mine,
    )
    mine = (up_weight, up_first, up_second)
    new_up = call(
        update_up, (1,),
        [full(4, part, 3 * heads + units)] + [full(*x.shape) for x in mine],
        [full(*x.shape) for x in mine], [struct(x.shape, WIDE) for x in mine], (back_cut,) + mine,
    )
    new_dense = adamw(dense_weight, dense_first, dense_second, owned_dense, 0.2, WEIGHT_DECAY)
    new_down = adamw(down_weight, down_first, down_second, owned_down, 0.03, WEIGHT_DECAY)
    new_qkv_bias = adamw(qkv_bias, qkv_bias_first, qkv_bias_second, owned_qkv_bias, 0.5, 0.0)
    new_up_bias = adamw(up_bias, up_bias_first, up_bias_second, owned_up_bias, 0.5, 0.0)
    new_vectors = adamw(vectors, vector_first, vector_second, owned_vectors, 0.5, 0.0)
    return (output, input_grad, *new_qkv, *new_dense, *new_up, *new_down, *new_qkv_bias, *new_up_bias, *new_vectors)


def solution(mesh):
    mesh = Mesh(mesh.devices.reshape(4, 2, 4, 2, 2), ("y", "xh", "z", "c", "mp"))
    dp = ("y", "xh", "z", "c")
    both = ("mp",) + dp
    weights = (P(None, dp, "mp"),) * 3 + (P(both, None),) * 3 + (P(dp, "mp"),) * 3 + (P(both, None),) * 3
    smalls = (P(None, both),) * 3 + (P(both),) * 3 + (P(None, dp),) * 3
    rows = P(dp, None)
    in_specs = (rows, rows, rows) + weights + smalls
    out_specs = (rows, rows) + weights + smalls
    return jax.shard_map(local, mesh=mesh, in_specs=in_specs, out_specs=out_specs, check_vma=False)
```
